32 devices in a mesh: az: 16 (over z, y, x), rad: 2 (over core).
Axes of the slice: x: 2, y: 2, z: 4, core: 2. Of those that a mesh axis runs over, the one named last changes fastest.
Arguments:
- fields: float32 [5, 2, 192, 4096], P(None, None, 'rad', 'az'), as said below
- shifts: int32 [192], P('rad'), may hold values from 0 to 4095, as said below
- cycle_area: float32 [192], P('rad'), may hold values from 0.5 to 2
- gravity: float32 [192], P('rad'), may hold values from 0.00052083336 to 0.0052083335
- kappa_az: float32 [192], P('rad'), may hold values from 0.05 to 0.24
- kappa_rad: float32 [192], P('rad'), may hold values from 0.05 to 0.24
Outputs:
- updated: float32 [5, 2, 192, 4096], P(None, None, 'rad', 'az')
- enclosed: float32 [192], P('rad')
The draws below stay inside these ranges and needn't reach their ends.
Inputs may be any that keep to these rules, and one draw needn't show every extreme that they name: shifts[r] is the whole number of cells by which row r moves toward higher azimuth. fields[0] is positive.
All inputs are finite; a program needn't handle non-finite values.
Results may differ from the reference program's by a relative error of at most 0.00002.
Values sent between devices are 32-bit elements; how exact they have to be, the bound alone decides.
A program may use at most 64 MiB of HBM per device.

```python
import math
import jax
import jax.numpy as jnp
from jax import lax

FIELDS = 5
LAYERS = 2
NR = 192
NA = 4096


def draw_fields(key, part):
    key = jax.random.fold_in(key, 7)
    key_rough, key_other = jax.random.split(key, 2)
    ramp = 1.0 + 2.0 * jnp.arange(NA, dtype=jnp.float32) / NA
    density = ramp * jax.random.uniform(key_rough, (LAYERS, NR, NA), jnp.float32, 0.5, 1.5)
    others = jax.random.normal(key_other, (FIELDS - 1, LAYERS, NR, NA), jnp.float32)
    return jnp.concatenate([density[None], others], axis=0)


def draw_shifts(key, part):
    key = jax.random.fold_in(key, 11)
    values = jax.random.randint(key, (NR,), 0, NA, jnp.int32)
    return values.at[0].set(NA - 1).at[1].set(0)


def block_scale(rng, dims, cuts, least, largest):
    def one(position, parts):
        draws = jax.random.uniform(jax.random.fold_in(jax.random.fold_in(rng, 6), position), (parts,), jnp.float32, least / len(cuts), largest / len(cuts))
        return jnp.repeat(jnp.exp(draws), dims[position] // parts).reshape((-1,) + (1,) * (len(dims) - position - 1))

    factor_of = one(*cuts[0])
    for cut in cuts[1:]:
        factor_of = factor_of * one(*cut)
    return factor_of


def setup_inputs(seed: int = 0) -> dict:
    splits = jax.random.split(jax.random.key(seed), 7)
    return {
        "fields": draw_fields(jax.random.fold_in(splits[6], 71), 0),
        "shifts": draw_shifts(jax.random.fold_in(splits[6], 71), 0),
        "cycle_area": jnp.clip(jnp.exp(math.log(2.0) - 1.3862944 * jax.random.uniform(splits[2], (NR,), jnp.float32) ** block_scale(splits[2], (NR,), ((0, 2),), -0.2, 0.2)), 0.5, 2.0),
        "gravity": jnp.clip(jnp.exp(math.log(0.0052083335) - 2.3025851 * jax.random.uniform(splits[3], (NR,), jnp.float32) ** block_scale(splits[3], (NR,), ((0, 2),), -0.2, 0.2)), 0.00052083336, 0.0052083335),
        "kappa_az": jnp.clip(0.05 + 0.19 * jax.random.uniform(splits[4], (NR,), jnp.float32) ** block_scale(splits[4], (NR,), ((0, 2),), -0.2, 0.2), 0.05, 0.24),
        "kappa_rad": jnp.clip(0.05 + 0.19 * jax.random.uniform(splits[5], (NR,), jnp.float32) ** block_scale(splits[5], (NR,), ((0, 2),), -0.2, 0.2), 0.05, 0.24),
    }


star_mass = 1.0


def shift_field(field, shifts):
    cell_index = (jnp.arange(NA, dtype=jnp.int32)[None, :] - shifts[:, None]) % NA
    cell_index = jnp.broadcast_to(cell_index[None], field.shape)
    return jnp.take_along_axis(field, cell_index, axis=2)


def reference(fields, shifts, cycle_area, gravity, kappa_az, kappa_rad):
    density = fields[0]
    row_mass = cycle_area * jnp.sum(density, axis=(0, 2)) / (2.0 * NA)
    before = jnp.cumsum(row_mass) - row_mass
    enclosed = star_mass + before + 0.5 * row_mass
    pull_rate = (gravity * enclosed)[None, :, None]
    momentum = fields[1] - pull_rate * density
    energy = fields[3] - pull_rate * fields[1]
    sourced = jnp.stack([density, momentum, fields[2], energy, fields[4]])
    advected = lax.map(lambda field: shift_field(field, shifts), sourced)
    beside_all = jnp.roll(advected, 1, axis=3) + jnp.roll(advected, -1, axis=3) - 2.0 * advected
    padded = jnp.pad(advected, ((0, 0), (0, 0), (1, 1), (0, 0)))
    across = padded[:, :, 2:] + padded[:, :, :-2] - 2.0 * advected
    updated = advected + kappa_az[None, None, :, None] * beside_all + kappa_rad[None, None, :, None] * across
    return updated, enclosed
```

```python
import functools

import jax
import jax.numpy as jnp
from jax import lax
from jax.experimental import pallas as pl
from jax.experimental.pallas import tpu as pltpu
from jax.sharding import PartitionSpec as P

MESH = pl.DeviceIdType.MESH
SUB = 8
LANES = 128
star_mass = 1.0


def kernel(
    n, m, layers,
    fields, shifts, area, gravity, kappa_az, kappa_rad,
    out, enclosed_out,
    win, wout, adv, edge_out, edge_in, mass, total, shift_table, halo_in,
    send1, recv1, send2, recv2, mass_send, mass_recv, total_send, total_recv,
    edge_send, edge_recv, halo_send, halo_recv,
):
    slabs, rows, cols = fields.shape
    per_slab = rows // SUB
    groups = slabs * per_slab
    chunks = -(-groups // n)
    last = groups - n * (chunks - 1)
    me = lax.axis_index("az")
    ring = lax.axis_index("rad")

    def peer(step):
        return lax.rem(me + step, n)

    def rad_peer(step):
        return lax.rem(ring + step, m)

    def place(group):
        slab = lax.rem(group, slabs)
        block = lax.rem(per_slab - lax.div(group, slabs), per_slab)
        return slab, pl.ds(pl.multiple_of(block * SUB, SUB), SUB)

    def last_of(device):
        index = lax.div(device * last + n - 1, n)
        held = (index < last) & (lax.div(index * n, last) == device)
        return held, n * (chunks - 1) + index

    def to_peer(src, dst, send, recv, device):
        return pltpu.make_async_remote_copy(
            src_ref=src, dst_ref=dst, send_sem=send, recv_sem=recv,
            device_id={"az": device}, device_id_type=MESH,
        )

    def to_rad(src, dst, send, recv, device):
        return pltpu.make_async_remote_copy(
            src_ref=src, dst_ref=dst, send_sem=send, recv_sem=recv,
            device_id={"rad": device}, device_id_type=MESH,
        )

    def drain(ref, sem):
        pltpu.make_async_copy(ref, ref, sem).wait()

    def pieces(count):
        return win.at[0, pl.ds(0, count)]

    barrier = pltpu.get_barrier_semaphore()

    def greet(step, _):
        pl.semaphore_signal(barrier, inc=1, device_id={"az": peer(step)}, device_id_type=MESH)
        return 0

    def greet_rad(step, _):
        pl.semaphore_signal(barrier, inc=1, device_id={"rad": rad_peer(step)}, device_id_type=MESH)
        return 0

    lax.fori_loop(1, n, greet, 0)
    lax.fori_loop(1, m, greet_rad, 0)

    row_at = lax.broadcasted_iota(jnp.int32, (rows, LANES), 0)
    lane_at = lax.broadcasted_iota(jnp.int32, (rows, LANES), 1)
    square_row = lax.broadcasted_iota(jnp.int32, (rows, rows), 0)
    square_lane = lax.broadcasted_iota(jnp.int32, (rows, rows), 1)

    def as_column(line):
        return jnp.sum(jnp.where(square_row == square_lane, line, 0.0), axis=1, keepdims=True)

    density = fields[0]
    for z in range(1, layers):
        density = density + fields[z]
    local = jnp.sum(density, axis=1, keepdims=True)
    mass[me] = jnp.sum(jnp.where(row_at == lane_at, local, 0.0), axis=0, keepdims=True)

    pl.semaphore_wait(barrier, n - 1 + m - 1)

    def send_mass(step, _):
        to_peer(mass.at[me], mass.at[me], mass_send, mass_recv, peer(step)).start()
        return 0

    lax.fori_loop(1, n, send_mass, 0)

    def send_rows(chunk, _):
        def one(step, _):
            device = peer(step)
            slab, block = place(n * chunk + device)
            to_peer(
                fields.at[slab, block], win.at[chunk, me], send1.at[chunk], recv1.at[chunk], device
            ).start()
            return 0

        return lax.fori_loop(1, n, one, 0)

    lax.fori_loop(0, chunks - 1, send_rows, 0)

    def send_last(step, _):
        device = peer(step)
        held, group = last_of(device)

        @pl.when(held)
        def _():
            slab, block = place(group)
            to_peer(
                fields.at[slab, block], win.at[chunks - 1, me],
                send1.at[chunks - 1], recv1.at[chunks - 1], device,
            ).start()

        return 0

    lax.fori_loop(1, n, send_last, 0)

    drain(mass.at[pl.ds(0, n - 1)], mass_recv)
    cycle_mass = jnp.sum(mass[...], axis=0)[:, :rows]
    row_mass = area[...] * cycle_mass / (2.0 * (n * cols))
    block_mass = jnp.sum(row_mass, axis=1, keepdims=True)
    total[ring] = jnp.broadcast_to(block_mass, (1, LANES))

    def send_total(step, _):
        to_rad(total.at[ring], total.at[ring], total_send, total_recv, rad_peer(step)).start()
        return 0

    lax.fori_loop(1, m, send_total, 0)
    before = jnp.sum(jnp.where(square_lane < square_row, row_mass, 0.0), axis=1, keepdims=True)
    own = as_column(row_mass)
    drain(total.at[pl.ds(0, m - 1)], total_recv)
    rank = lax.broadcasted_iota(jnp.int32, (m, 1, LANES), 0)
    offset = jnp.sum(jnp.where(rank < ring, total[...], 0.0), axis=0)[:, :1]
    enclosed = star_mass + offset + before + 0.5 * own
    enclosed_out[...] = jnp.sum(jnp.where(square_row == square_lane, enclosed, 0.0), axis=0, keepdims=True)
    pull = as_column(gravity[...]) * enclosed

    shift_column = as_column(shifts[...].astype(jnp.float32)).astype(jnp.int32)
    shift_rows = jnp.broadcast_to(shift_column, (rows, LANES))
    shift_table[...] = shift_rows

    cells = n * cols
    small = lax.broadcasted_iota(jnp.int32, (SUB, LANES), 1)

    def roll_chunk(chunk, group):
        slab, block = place(group)
        win[chunk, me] = fields[slab, block, :]
        amount = shift_table[block, :]
        amount = amount[:, :1]
        row = jnp.concatenate([win[chunk, i] for i in range(n)], axis=1)
        for bit in range((cells - 1).bit_length()):
            rolled = pltpu.roll(row, 1 << bit, axis=1)
            row = jnp.where((amount >> bit) & 1 == 1, rolled, row)
        for i in range(n):
            wout[chunk, i] = row[:, i * cols:(i + 1) * cols]
        adv[slab, block, :] = wout[chunk, me]

        def back(step, _):
            device = peer(step)
            to_peer(
                wout.at[chunk, device], adv.at[slab, block], send2.at[chunk], recv2.at[chunk], device
            ).start()
            return 0

        lax.fori_loop(1, n, back, 0)
        for i in range(n):
            low = (i * cols - 1) % cells
            high = (i * cols + cols) % cells
            edge_out[i] = jnp.where(
                small == 2 * chunk, row[:, low:low + 1],
                jnp.where(small == 2 * chunk + 1, row[:, high:high + 1], edge_out[i]),
            )

    edge_out[...] = jnp.zeros(edge_out.shape, jnp.float32)

    def turn(chunk, _):
        drain(pieces(n - 1), recv1.at[chunk])
        roll_chunk(chunk, n * chunk + me)
        return 0

    lax.fori_loop(0, chunks - 1, turn, 0)
    held, group = last_of(me)

    @pl.when(held)
    def _():
        drain(pieces(n - 1), recv1.at[chunks - 1])
        roll_chunk(chunks - 1, group)

    edge_in[me] = edge_out[me]

    def send_edges(step, _):
        device = peer(step)
        to_peer(edge_out.at[device], edge_in.at[me], edge_send, edge_recv, device).start()
        return 0

    lax.fori_loop(1, n, send_edges, 0)

    def wait_back(chunk, _):
        drain(pieces(n - 1), recv2.at[chunk])
        return 0

    def wait_last(sem):
        @pl.when(held)
        def _():
            drain(pieces(last - 1), sem)

        @pl.when(jnp.logical_not(held))
        def _():
            drain(pieces(last), sem)

    early = min((2 * slabs - 1) // n + 1, chunks - 1)
    lax.fori_loop(0, early, wait_back, 0)

    for side, at in ((1, 0), (2, rows - 1)):
        rate = pull[at:at + 1, :]
        for slab in range(slabs):
            line = adv[slab, at:at + 1, :]
            if slab // layers in (1, 3):
                below = slab - layers if slab // layers == 1 else slab - 2 * layers
                line = line - rate * adv[below, at:at + 1, :]
            halo_in[side - 1, slab:slab + 1, :] = line
    to_rad(halo_in.at[0], halo_in.at[2], halo_send.at[0], halo_recv.at[0], rad_peer(m - 1)).start()
    to_rad(halo_in.at[1], halo_in.at[3], halo_send.at[1], halo_recv.at[1], rad_peer(1)).start()

    lax.fori_loop(early, chunks - 1, wait_back, 0)
    wait_last(recv2.at[chunks - 1])
    drain(edge_in.at[pl.ds(0, n - 1)], edge_recv)
    drain(halo_in.at[0], halo_recv.at[0])
    drain(halo_in.at[1], halo_recv.at[1])

    along = as_column(kappa_az[...])
    across = as_column(kappa_rad[...])
    wide_row = lax.broadcasted_iota(jnp.int32, (rows, cols), 0)
    wide_lane = lax.broadcasted_iota(jnp.int32, (rows, cols), 1)
    inner = ring > 0
    outer = ring < m - 1

    def ends(slab):
        sides = ([], [])
        for block in range(per_slab):
            index = ((per_slab - block) % per_slab) * slabs + slab
            chunk = index // n
            device = index % n if chunk < chunks - 1 else (index - n * chunk) * n // last
            for side in range(2):
                sides[side].append(edge_in[device, :, 2 * chunk + side:2 * chunk + side + 1])
        return jnp.concatenate(sides[0], axis=0), jnp.concatenate(sides[1], axis=0)

    for slab in range(slabs):
        here = adv[slab]
        left, right = ends(slab)
        if slab // layers in (1, 3):
            below = slab - layers if slab // layers == 1 else slab - 2 * layers
            here = here - pull * adv[below]
            other_left, other_right = ends(below)
            left = left - pull * other_left
            right = right - pull * other_right
        top = jnp.where(inner, halo_in[3, slab:slab + 1, :], 0.0)
        bottom = jnp.where(outer, halo_in[2, slab:slab + 1, :], 0.0)
        lower = jnp.where(wide_lane == 0, left, pltpu.roll(here, 1, axis=1))
        upper = jnp.where(wide_lane == cols - 1, right, pltpu.roll(here, cols - 1, axis=1))
        above = jnp.where(wide_row == 0, top, pltpu.roll(here, 1, axis=0))
        beneath = jnp.where(wide_row == rows - 1, bottom, pltpu.roll(here, rows - 1, axis=0))
        twice = 2.0 * here
        out[slab] = (
            here + along * (lower + upper - twice) + across * (beneath + above - twice)
        )

    drain(mass.at[pl.ds(0, n - 1)], mass_send)
    drain(total.at[pl.ds(0, m - 1)], total_send)
    drain(edge_in.at[pl.ds(0, n - 1)], edge_send)
    drain(halo_in.at[0], halo_send.at[0])
    drain(halo_in.at[1], halo_send.at[1])

    def wait_sent(chunk, _):
        drain(pieces(n - 1), send1.at[chunk])
        drain(pieces(n - 1), send2.at[chunk])
        return 0

    lax.fori_loop(0, chunks - 1, wait_sent, 0)
    wait_last(send1.at[chunks - 1])

    @pl.when(held)
    def _():
        drain(pieces(n - 1), send2.at[chunks - 1])


def shards(n, m, fields, shifts, area, gravity, kappa_az, kappa_rad):
    kinds, layers, rows, cols = fields.shape
    slabs = kinds * layers
    chunks = -(-(slabs * (rows // SUB)) // n)
    line = (1, rows)
    f32 = jnp.float32
    dma = pltpu.SemaphoreType.DMA
    vmem = pl.BlockSpec(memory_space=pltpu.VMEM)
    slab_pad = -(-slabs // SUB) * SUB
    updated, enclosed = pl.pallas_call(
        functools.partial(kernel, n, m, layers),
        out_shape=(
            jax.ShapeDtypeStruct((slabs, rows, cols), f32),
            jax.ShapeDtypeStruct(line, f32),
        ),
        in_specs=[vmem] * 6,
        out_specs=(vmem, vmem),
        scratch_shapes=[
            pltpu.VMEM((chunks, n, SUB, cols), f32),
            pltpu.VMEM((chunks, n, SUB, cols), f32),
            pltpu.VMEM((slabs, rows, cols), f32),
            pltpu.VMEM((n, SUB, LANES), f32),
            pltpu.VMEM((n, SUB, LANES), f32),
            pltpu.VMEM((n, 1, LANES), f32),
            pltpu.VMEM((m, 1, LANES), f32),
            pltpu.VMEM((rows, LANES), jnp.int32),
            pltpu.VMEM((4, slab_pad, cols), f32),
            dma((chunks,)), dma((chunks,)), dma((chunks,)), dma((chunks,)),
            dma, dma, dma, dma, dma, dma, dma((2,)), dma((2,)),
        ],
        compiler_params=pltpu.CompilerParams(
            collective_id=0, has_side_effects=True, vmem_limit_bytes=32 * 1024 * 1024
        ),
    )(
        fields.reshape(slabs, rows, cols), shifts.reshape(line), area.reshape(line),
        gravity.reshape(line), kappa_az.reshape(line), kappa_rad.reshape(line),
    )
    return updated.reshape(fields.shape), enclosed.reshape(rows)


def solution(mesh):
    placed = (P(None, None, "rad", "az"), P("rad"), P("rad"), P("rad"), P("rad"), P("rad"))
    return jax.shard_map(
        functools.partial(shards, mesh.shape["az"], mesh.shape["rad"]),
        mesh=mesh,
        in_specs=placed,
        out_specs=(P(None, None, "rad", "az"), P("rad")),
        check_vma=False,
    )
```

```python
import functools

import jax
import jax.numpy as jnp
from jax import lax
from jax.experimental import pallas as pl
from jax.experimental.pallas import tpu as pltpu
from jax.sharding import PartitionSpec as P

MESH = pl.DeviceIdType.MESH
SUB = 8
LANES = 128
star_mass = 1.0


def kernel(
    n, m, layers,
    source, shifts_in, area_in, gravity_in, kappa_az_in, kappa_rad_in,
    out, enclosed_out,
    fields, shifts, area, gravity, kappa_az, kappa_rad, load_sem,
    win, wout, adv, edge_sum, edge_out, edge_in, mass, total, shift_table, halo_in,
    send1, recv1, send2, recv2, mass_send, mass_recv, total_send, total_recv,
    edge_send, edge_recv, halo_send, halo_recv,
):
    slabs, rows, cols = fields.shape
    per_slab = rows // SUB
    groups = slabs * per_slab
    chunks = -(-groups // n)
    last = groups - n * (chunks - 1)
    me = lax.axis_index("az")
    ring = lax.axis_index("rad")

    def peer(step):
        return lax.rem(me + step, n)

    def rad_peer(step):
        return lax.rem(ring + step, m)

    def place(group):
        slab = lax.rem(group, slabs)
        block = lax.rem(per_slab - lax.div(group, slabs), per_slab)
        return slab, pl.ds(pl.multiple_of(block * SUB, SUB), SUB)

    def owner(index):
        if n == 2 * last:
            return 2 * index + lax.rem(lax.div(index, 2) + index, 2)
        return lax.div(index * n + n - 1, last)

    def last_of(device):
        index = lax.div(device * last, n)
        held = owner(index) == device
        return held, n * (chunks - 1) + index

    def to_peer(src, dst, send, recv, device):
        return pltpu.make_async_remote_copy(
            src_ref=src, dst_ref=dst, send_sem=send, recv_sem=recv,
            device_id={"az": device}, device_id_type=MESH,
        )

    def to_rad(src, dst, send, recv, device):
        return pltpu.make_async_remote_copy(
            src_ref=src, dst_ref=dst, send_sem=send, recv_sem=recv,
            device_id={"rad": device}, device_id_type=MESH,
        )

    def drain(ref, sem):
        pltpu.make_async_copy(ref, ref, sem).wait()

    def pieces(count):
        return win.at[0, pl.ds(0, count)]

    loads = [
        pltpu.make_async_copy(here, there, load_sem.at[i])
        for i, (here, there) in enumerate((
            (source, fields), (shifts_in, shifts), (area_in, area),
            (gravity_in, gravity), (kappa_az_in, kappa_az), (kappa_rad_in, kappa_rad),
        ))
    ]
    for load in loads:
        load.start()

    barrier = pltpu.get_barrier_semaphore()

    def greet(step, _):
        pl.semaphore_signal(barrier, inc=1, device_id={"az": peer(step)}, device_id_type=MESH)
        return 0

    def greet_rad(step, _):
        pl.semaphore_signal(barrier, inc=1, device_id={"rad": rad_peer(step)}, device_id_type=MESH)
        return 0

    lax.fori_loop(1, n, greet, 0)
    lax.fori_loop(1, m, greet_rad, 0)

    row_at = lax.broadcasted_iota(jnp.int32, (rows, LANES), 0)
    lane_at = lax.broadcasted_iota(jnp.int32, (rows, LANES), 1)
    square_row = lax.broadcasted_iota(jnp.int32, (rows, rows), 0)
    square_lane = lax.broadcasted_iota(jnp.int32, (rows, rows), 1)

    def as_column(line):
        return jnp.sum(jnp.where(square_row == square_lane, line, 0.0), axis=1, keepdims=True)

    for load in loads:
        load.wait()
    density = fields[0]
    for z in range(1, layers):
        density = density + fields[z]
    local = jnp.sum(density, axis=1, keepdims=True)
    mass[me] = jnp.sum(jnp.where(row_at == lane_at, local, 0.0), axis=0, keepdims=True)

    pl.semaphore_wait(barrier, n - 1 + m - 1)

    def send_mass(step, _):
        to_peer(mass.at[me], mass.at[me], mass_send, mass_recv, peer(step)).start()
        return 0

    lax.fori_loop(1, n, send_mass, 0)

    def send_rows(chunk, _):
        def one(step, _):
            device = peer(step)
            slab, block = place(n * chunk + device)
            to_peer(
                source.at[slab, block], win.at[chunk, me], send1.at[chunk], recv1.at[chunk], device
            ).start()
            return 0

        return lax.fori_loop(1, n, one, 0)

    lax.fori_loop(0, chunks - 1, send_rows, 0)

    def send_last(step, _):
        device = peer(step)
        held, group = last_of(device)

        @pl.when(held)
        def _():
            slab, block = place(group)
            to_peer(
                source.at[slab, block], win.at[chunks - 1, me],
                send1.at[chunks - 1], recv1.at[chunks - 1], device,
            ).start()

        return 0

    lax.fori_loop(1, n, send_last, 0)

    shift_column = as_column(shifts[...].astype(jnp.float32)).astype(jnp.int32)
    shift_rows = jnp.broadcast_to(shift_column, (rows, LANES))
    shift_table[...] = shift_rows

    cells = n * cols
    spots = 2 * SUB
    small = lax.broadcasted_iota(jnp.int32, (SUB, LANES), 1) - lax.broadcasted_iota(jnp.int32, (SUB, LANES), 0)

    def roll_chunk(chunk, group):
        slab, block = place(group)
        win[chunk, me] = fields[slab, block, :]
        amount = shift_table[block, :]
        amount = amount[:, :1]
        row = jnp.concatenate([win[chunk, i] for i in range(n)], axis=1)
        for bit in range((cells - 1).bit_length()):
            rolled = pltpu.roll(row, 1 << bit, axis=1)
            row = jnp.where((amount >> bit) & 1 == 1, rolled, row)
        for i in range(n):
            wout[chunk, i] = row[:, i * cols:(i + 1) * cols]
        adv[slab, block, :] = wout[chunk, me]

        def back(step, _):
            device = peer(step)
            to_peer(
                wout.at[chunk, device], adv.at[slab, block], send2.at[chunk], recv2.at[chunk], device
            ).start()
            return 0

        lax.fori_loop(1, n, back, 0)
        for i in range(n):
            low = (i * cols - 1) % cells
            high = (i * cols + cols) % cells
            edge_sum[i] = jnp.where(
                small == spots * chunk, row[:, low:low + 1],
                jnp.where(small == spots * chunk + SUB, row[:, high:high + 1], edge_sum[i]),
            )

    edge_sum[...] = jnp.zeros(edge_sum.shape, jnp.float32)

    def turn(chunk, _):
        drain(pieces(n - 1), recv1.at[chunk])
        roll_chunk(chunk, n * chunk + me)
        return 0

    lax.fori_loop(0, chunks - 1, turn, 0)
    held, group = last_of(me)

    @pl.when(held)
    def _():
        drain(pieces(n - 1), recv1.at[chunks - 1])
        roll_chunk(chunks - 1, group)

    edge_out[...] = jnp.sum(edge_sum[...], axis=1, keepdims=True)
    edge_in[me] = edge_out[me]

    def send_edges(step, _):
        device = peer(step)
        to_peer(edge_out.at[device], edge_in.at[me], edge_send, edge_recv, device).start()
        return 0

    lax.fori_loop(1, n, send_edges, 0)

    def wait_back(chunk, _):
        drain(pieces(n - 1), recv2.at[chunk])
        return 0

    def wait_last(sem):
        @pl.when(held)
        def _():
            drain(pieces(last - 1), sem)

        @pl.when(jnp.logical_not(held))
        def _():
            drain(pieces(last), sem)

    drain(mass.at[pl.ds(0, n - 1)], mass_recv)
    cycle_mass = jnp.sum(mass[...], axis=0)[:, :rows]
    row_mass = area[...] * cycle_mass / (2.0 * (n * cols))
    block_mass = jnp.sum(row_mass, axis=1, keepdims=True)
    total[ring] = jnp.broadcast_to(block_mass, (1, LANES))

    def send_total(step, _):
        to_rad(total.at[ring], total.at[ring], total_send, total_recv, rad_peer(step)).start()
        return 0

    lax.fori_loop(1, m, send_total, 0)
    before = jnp.sum(jnp.where(square_lane < square_row, row_mass, 0.0), axis=1, keepdims=True)
    own = as_column(row_mass)
    drain(total.at[pl.ds(0, m - 1)], total_recv)
    rank = lax.broadcasted_iota(jnp.int32, (m, 1, LANES), 0)
    offset = jnp.sum(jnp.where(rank < ring, total[...], 0.0), axis=0)[:, :1]
    enclosed = star_mass + offset + before + 0.5 * own
    enclosed_out[...] = jnp.sum(jnp.where(square_row == square_lane, enclosed, 0.0), axis=0, keepdims=True)
    pull = as_column(gravity[...]) * enclosed

    early = min((2 * slabs - 1) // n + 1, chunks - 1)
    lax.fori_loop(0, early, wait_back, 0)

    for side, at in ((1, 0), (2, rows - 1)):
        rate = pull[at:at + 1, :]
        for slab in range(slabs):
            line = adv[slab, at:at + 1, :]
            if slab // layers in (1, 3):
                below = slab - layers if slab // layers == 1 else slab - 2 * layers
                line = line - rate * adv[below, at:at + 1, :]
            halo_in[side - 1, slab:slab + 1, :] = line
    to_rad(halo_in.at[0], halo_in.at[2], halo_send.at[0], halo_recv.at[0], rad_peer(m - 1)).start()
    to_rad(halo_in.at[1], halo_in.at[3], halo_send.at[1], halo_recv.at[1], rad_peer(1)).start()

    lax.fori_loop(early, chunks - 1, wait_back, 0)
    wait_last(recv2.at[chunks - 1])
    drain(edge_in.at[pl.ds(0, n - 1)], edge_recv)
    drain(halo_in.at[0], halo_recv.at[0])
    drain(halo_in.at[1], halo_recv.at[1])

    along = as_column(kappa_az[...])
    across = as_column(kappa_rad[...])
    wide_row = lax.broadcasted_iota(jnp.int32, (rows, cols), 0)
    wide_lane = lax.broadcasted_iota(jnp.int32, (rows, cols), 1)
    inner = ring > 0
    outer = ring < m - 1

    def static_owner(index):
        if n == 2 * last:
            return 2 * index + (index // 2 + index) % 2
        return (index * n + n - 1) // last

    def ends(slab):
        sides = ([], [])
        for block in range(per_slab):
            index = ((per_slab - block) % per_slab) * slabs + slab
            chunk = index // n
            device = index % n if chunk < chunks - 1 else static_owner(index - n * chunk)
            line = edge_in[device]
            for side in range(2):
                spot = jnp.where(small == spots * chunk + SUB * side, line, 0.0)
                sides[side].append(jnp.sum(spot, axis=1, keepdims=True))
        return jnp.concatenate(sides[0], axis=0), jnp.concatenate(sides[1], axis=0)

    edges = [ends(slab) for slab in range(slabs)]
    for slab in range(slabs):
        here = adv[slab]
        left, right = edges[slab]
        if slab // layers in (1, 3):
            below = slab - layers if slab // layers == 1 else slab - 2 * layers
            here = here - pull * adv[below]
            other_left, other_right = edges[below]
            left = left - pull * other_left
            right = right - pull * other_right
        top = jnp.where(inner, halo_in[3, slab:slab + 1, :], 0.0)
        bottom = jnp.where(outer, halo_in[2, slab:slab + 1, :], 0.0)
        lower = jnp.where(wide_lane == 0, left, pltpu.roll(here, 1, axis=1))
        upper = jnp.where(wide_lane == cols - 1, right, pltpu.roll(here, cols - 1, axis=1))
        above = jnp.where(wide_row == 0, top, pltpu.roll(here, 1, axis=0))
        beneath = jnp.where(wide_row == rows - 1, bottom, pltpu.roll(here, rows - 1, axis=0))
        twice = 2.0 * here
        out[slab] = (
            here + along * (lower + upper - twice) + across * (beneath + above - twice)
        )

    drain(mass.at[pl.ds(0, n - 1)], mass_send)
    drain(total.at[pl.ds(0, m - 1)], total_send)
    drain(edge_in.at[pl.ds(0, n - 1)], edge_send)
    drain(halo_in.at[0], halo_send.at[0])
    drain(halo_in.at[1], halo_send.at[1])

    def wait_sent(chunk, _):
        drain(pieces(n - 1), send1.at[chunk])
        drain(pieces(n - 1), send2.at[chunk])
        return 0

    lax.fori_loop(0, chunks - 1, wait_sent, 0)
    wait_last(send1.at[chunks - 1])

    @pl.when(held)
    def _():
        drain(pieces(n - 1), send2.at[chunks - 1])


def shards(n, m, fields, shifts, area, gravity, kappa_az, kappa_rad):
    kinds, layers, rows, cols = fields.shape
    slabs = kinds * layers
    chunks = -(-(slabs * (rows // SUB)) // n)
    line = (1, rows)
    f32 = jnp.float32
    dma = pltpu.SemaphoreType.DMA
    vmem = pl.BlockSpec(memory_space=pltpu.VMEM)
    hbm = pl.BlockSpec(memory_space=pltpu.HBM)
    assert 2 * SUB * chunks <= LANES
    slab_pad = -(-slabs // SUB) * SUB
    updated, enclosed = pl.pallas_call(
        functools.partial(kernel, n, m, layers),
        out_shape=(
            jax.ShapeDtypeStruct((slabs, rows, cols), f32),
            jax.ShapeDtypeStruct(line, f32),
        ),
        in_specs=[hbm] * 6,
        out_specs=(vmem, vmem),
        scratch_shapes=[
            pltpu.VMEM((slabs, rows, cols), f32),
            pltpu.VMEM(line, jnp.int32),
            pltpu.VMEM(line, f32), pltpu.VMEM(line, f32), pltpu.VMEM(line, f32), pltpu.VMEM(line, f32),
            dma((6,)),
            pltpu.VMEM((chunks, n, SUB, cols), f32),
            pltpu.VMEM((chunks, n, SUB, cols), f32),
            pltpu.VMEM((slabs, rows, cols), f32),
            pltpu.VMEM((n, SUB, LANES), f32),
            pltpu.VMEM((n, 1, LANES), f32),
            pltpu.VMEM((n, 1, LANES), f32),
            pltpu.VMEM((n, 1, LANES), f32),
            pltpu.VMEM((m, 1, LANES), f32),
            pltpu.VMEM((rows, LANES), jnp.int32),
            pltpu.VMEM((4, slab_pad, cols), f32),
            dma((chunks,)), dma((chunks,)), dma((chunks,)), dma((chunks,)),
            dma, dma, dma, dma, dma, dma, dma((2,)), dma((2,)),
        ],
        compiler_params=pltpu.CompilerParams(
            collective_id=0, has_side_effects=True, vmem_limit_bytes=32 * 1024 * 1024
        ),
    )(
        fields.reshape(slabs, rows, cols), shifts.reshape(line), area.reshape(line),
        gravity.reshape(line), kappa_az.reshape(line), kappa_rad.reshape(line),
    )
    return updated.reshape(fields.shape), enclosed.reshape(rows)


def solution(mesh):
    placed = (P(None, None, "rad", "az"), P("rad"), P("rad"), P("rad"), P("rad"), P("rad"))
    return jax.shard_map(
        functools.partial(shards, mesh.shape["az"], mesh.shape["rad"]),
        mesh=mesh,
        in_specs=placed,
        out_specs=(P(None, None, "rad", "az"), P("rad")),
        check_vma=False,
    )
```

```python
import functools

import jax
import jax.numpy as jnp
from jax import lax
from jax.experimental import pallas as pl
from jax.experimental.pallas import tpu as pltpu
from jax.sharding import PartitionSpec as P

MESH = pl.DeviceIdType.MESH
SUB = 8
LANES = 128
star_mass = 1.0


def kernel(
    n, m, layers,
    source, shifts_in, area_in, gravity_in, kappa_az_in, kappa_rad_in,
    out_hbm, enclosed_out,
    out, out_sem, fields, shifts, area, gravity, kappa_az, kappa_rad, load_sem,
    win, wout, adv, edge_sum, edge_out, edge_in, mass, total, shift_table, halo_in,
    send1, recv1, send2, recv2, mass_send, mass_recv, total_send, total_recv,
    edge_send, edge_recv, halo_send, halo_recv,
):
    slabs, rows, cols = fields.shape
    per_slab = rows // SUB
    groups = slabs * per_slab
    chunks = -(-groups // n)
    last = groups - n * (chunks - 1)
    me = lax.axis_index("az")
    ring = lax.axis_index("rad")

    def peer(step):
        return lax.rem(me + step, n)

    def far_peer(turn):
        odd = lax.rem(turn, 2)
        return peer(n // 2 + (lax.div(turn, 2) + odd) * (2 * odd - 1))

    def rad_peer(step):
        return lax.rem(ring + step, m)

    def place(group):
        slab = lax.rem(group, slabs)
        block = lax.rem(per_slab - lax.div(group, slabs), per_slab)
        return slab, pl.ds(pl.multiple_of(block * SUB, SUB), SUB)

    def owner(index):
        if n == 2 * last:
            return 2 * index + lax.rem(lax.div(index, 2) + index, 2)
        return lax.div(index * n + n - 1, last)

    def last_of(device):
        index = lax.div(device * last, n)
        held = owner(index) == device
        return held, n * (chunks - 1) + index

    def to_peer(src, dst, send, recv, device):
        return pltpu.make_async_remote_copy(
            src_ref=src, dst_ref=dst, send_sem=send, recv_sem=recv,
            device_id={"az": device}, device_id_type=MESH,
        )

    def to_rad(src, dst, send, recv, device):
        return pltpu.make_async_remote_copy(
            src_ref=src, dst_ref=dst, send_sem=send, recv_sem=recv,
            device_id={"rad": device}, device_id_type=MESH,
        )

    def drain(ref, sem):
        pltpu.make_async_copy(ref, ref, sem).wait()

    def pieces(count):
        return win.at[0, pl.ds(0, count)]

    loads = [
        pltpu.make_async_copy(here, there, load_sem.at[i])
        for i, (here, there) in enumerate((
            (source, fields), (shifts_in, shifts), (area_in, area),
            (gravity_in, gravity), (kappa_az_in, kappa_az), (kappa_rad_in, kappa_rad),
        ))
    ]
    for load in loads:
        load.start()

    barrier = pltpu.get_barrier_semaphore()

    def greet(step, _):
        pl.semaphore_signal(barrier, inc=1, device_id={"az": peer(step)}, device_id_type=MESH)
        return 0

    def greet_rad(step, _):
        pl.semaphore_signal(barrier, inc=1, device_id={"rad": rad_peer(step)}, device_id_type=MESH)
        return 0

    lax.fori_loop(1, n, greet, 0)
    lax.fori_loop(1, m, greet_rad, 0)

    row_at = lax.broadcasted_iota(jnp.int32, (rows, LANES), 0)
    lane_at = lax.broadcasted_iota(jnp.int32, (rows, LANES), 1)
    square_row = lax.broadcasted_iota(jnp.int32, (rows, rows), 0)
    square_lane = lax.broadcasted_iota(jnp.int32, (rows, rows), 1)

    def as_column(line):
        return jnp.sum(jnp.where(square_row == square_lane, line, 0.0), axis=1, keepdims=True)

    for load in loads:
        load.wait()
    density = fields[0]
    for z in range(1, layers):
        density = density + fields[z]
    local = jnp.sum(density, axis=1, keepdims=True)
    mass[me] = jnp.sum(jnp.where(row_at == lane_at, local, 0.0), axis=0, keepdims=True)

    pl.semaphore_wait(barrier, n - 1 + m - 1)

    def send_mass(step, _):
        to_peer(mass.at[me], mass.at[me], mass_send, mass_recv, peer(step)).start()
        return 0

    lax.fori_loop(1, n, send_mass, 0)

    def send_rows(chunk, _):
        def one(turn, _):
            device = far_peer(turn)
            slab, block = place(n * chunk + device)
            to_peer(
                source.at[slab, block], win.at[chunk, me], send1.at[chunk], recv1.at[chunk], device
            ).start()
            return 0

        return lax.fori_loop(0, n - 1, one, 0)

    lax.fori_loop(0, chunks - 1, send_rows, 0)

    def send_last(turn, _):
        device = far_peer(turn)
        held, group = last_of(device)

        @pl.when(held)
        def _():
            slab, block = place(group)
            to_peer(
                source.at[slab, block], win.at[chunks - 1, me],
                send1.at[chunks - 1], recv1.at[chunks - 1], device,
            ).start()

        return 0

    lax.fori_loop(0, n - 1, send_last, 0)

    shift_column = as_column(shifts[...].astype(jnp.float32)).astype(jnp.int32)
    shift_rows = jnp.broadcast_to(shift_column, (rows, LANES))
    shift_table[...] = shift_rows

    cells = n * cols
    spots = 2 * SUB
    small = lax.broadcasted_iota(jnp.int32, (SUB, LANES), 1) - lax.broadcasted_iota(jnp.int32, (SUB, LANES), 0)

    def roll_chunk(chunk, group):
        slab, block = place(group)
        win[chunk, me] = fields[slab, block, :]
        amount = shift_table[block, :]
        amount = amount[:, :1]
        row = jnp.concatenate([win[chunk, i] for i in range(n)], axis=1)
        for bit in range((cells - 1).bit_length()):
            rolled = pltpu.roll(row, 1 << bit, axis=1)
            row = jnp.where((amount >> bit) & 1 == 1, rolled, row)
        for i in range(n):
            wout[chunk, i] = row[:, i * cols:(i + 1) * cols]
        adv[slab, block, :] = wout[chunk, me]

        def back(turn, _):
            device = far_peer(turn)
            to_peer(
                wout.at[chunk, device], adv.at[slab, block], send2.at[chunk], recv2.at[chunk], device
            ).start()
            return 0

        lax.fori_loop(0, n - 1, back, 0)
        for i in range(n):
            low = (i * cols - 1) % cells
            high = (i * cols + cols) % cells
            edge_sum[i] = jnp.where(
                small == spots * chunk, row[:, low:low + 1],
                jnp.where(small == spots * chunk + SUB, row[:, high:high + 1], edge_sum[i]),
            )

    edge_sum[...] = jnp.zeros(edge_sum.shape, jnp.float32)

    def turn(chunk, _):
        drain(pieces(n - 1), recv1.at[chunk])
        roll_chunk(chunk, n * chunk + me)
        return 0

    lax.fori_loop(0, chunks - 1, turn, 0)
    held, group = last_of(me)

    @pl.when(held)
    def _():
        drain(pieces(n - 1), recv1.at[chunks - 1])
        roll_chunk(chunks - 1, group)

    edge_out[...] = jnp.sum(edge_sum[...], axis=1, keepdims=True)
    edge_in[me] = edge_out[me]

    def send_edges(step, _):
        device = peer(step)
        to_peer(edge_out.at[device], edge_in.at[me], edge_send, edge_recv, device).start()
        return 0

    lax.fori_loop(1, n, send_edges, 0)

    def wait_back(chunk, _):
        drain(pieces(n - 1), recv2.at[chunk])
        return 0

    def wait_last(sem):
        @pl.when(held)
        def _():
            drain(pieces(last - 1), sem)

        @pl.when(jnp.logical_not(held))
        def _():
            drain(pieces(last), sem)

    drain(mass.at[pl.ds(0, n - 1)], mass_recv)
    cycle_mass = jnp.sum(mass[...], axis=0)[:, :rows]
    row_mass = area[...] * cycle_mass / (2.0 * (n * cols))
    block_mass = jnp.sum(row_mass, axis=1, keepdims=True)
    total[ring] = jnp.broadcast_to(block_mass, (1, LANES))

    def send_total(step, _):
        to_rad(total.at[ring], total.at[ring], total_send, total_recv, rad_peer(step)).start()
        return 0

    lax.fori_loop(1, m, send_total, 0)
    before = jnp.sum(jnp.where(square_lane < square_row, row_mass, 0.0), axis=1, keepdims=True)
    own = as_column(row_mass)
    drain(total.at[pl.ds(0, m - 1)], total_recv)
    rank = lax.broadcasted_iota(jnp.int32, (m, 1, LANES), 0)
    offset = jnp.sum(jnp.where(rank < ring, total[...], 0.0), axis=0)[:, :1]
    enclosed = star_mass + offset + before + 0.5 * own
    enclosed_out[...] = jnp.sum(jnp.where(square_row == square_lane, enclosed, 0.0), axis=0, keepdims=True)
    pull = as_column(gravity[...]) * enclosed

    early = min((2 * slabs - 1) // n + 1, chunks - 1)
    lax.fori_loop(0, early, wait_back, 0)

    for side, at in ((1, 0), (2, rows - 1)):
        rate = pull[at:at + 1, :]
        for slab in range(slabs):
            line = adv[slab, at:at + 1, :]
            if slab // layers in (1, 3):
                below = slab - layers if slab // layers == 1 else slab - 2 * layers
                line = line - rate * adv[below, at:at + 1, :]
            halo_in[side - 1, slab:slab + 1, :] = line
    to_rad(halo_in.at[0], halo_in.at[2], halo_send.at[0], halo_recv.at[0], rad_peer(m - 1)).start()
    to_rad(halo_in.at[1], halo_in.at[3], halo_send.at[1], halo_recv.at[1], rad_peer(1)).start()

    lax.fori_loop(early, chunks - 1, wait_back, 0)
    wait_last(recv2.at[chunks - 1])
    drain(edge_in.at[pl.ds(0, n - 1)], edge_recv)
    drain(halo_in.at[0], halo_recv.at[0])
    drain(halo_in.at[1], halo_recv.at[1])

    along = as_column(kappa_az[...])
    across = as_column(kappa_rad[...])
    wide_row = lax.broadcasted_iota(jnp.int32, (rows, cols), 0)
    wide_lane = lax.broadcasted_iota(jnp.int32, (rows, cols), 1)
    inner = ring > 0
    outer = ring < m - 1

    def static_owner(index):
        if n == 2 * last:
            return 2 * index + (index // 2 + index) % 2
        return (index * n + n - 1) // last

    def ends(slab):
        sides = ([], [])
        for block in range(per_slab):
            index = ((per_slab - block) % per_slab) * slabs + slab
            chunk = index // n
            device = index % n if chunk < chunks - 1 else static_owner(index - n * chunk)
            line = edge_in[device]
            for side in range(2):
                spot = jnp.where(small == spots * chunk + SUB * side, line, 0.0)
                sides[side].append(jnp.sum(spot, axis=1, keepdims=True))
        return jnp.concatenate(sides[0], axis=0), jnp.concatenate(sides[1], axis=0)

    edges = [ends(slab) for slab in range(slabs)]
    for slab in range(slabs):
        here = adv[slab]
        left, right = edges[slab]
        if slab // layers in (1, 3):
            below = slab - layers if slab // layers == 1 else slab - 2 * layers
            here = here - pull * adv[below]
            other_left, other_right = edges[below]
            left = left - pull * other_left
            right = right - pull * other_right
        top = jnp.where(inner, halo_in[3, slab:slab + 1, :], 0.0)
        bottom = jnp.where(outer, halo_in[2, slab:slab + 1, :], 0.0)
        lower = jnp.where(wide_lane == 0, left, pltpu.roll(here, 1, axis=1))
        upper = jnp.where(wide_lane == cols - 1, right, pltpu.roll(here, cols - 1, axis=1))
        above = jnp.where(wide_row == 0, top, pltpu.roll(here, 1, axis=0))
        beneath = jnp.where(wide_row == rows - 1, bottom, pltpu.roll(here, rows - 1, axis=0))
        twice = 2.0 * here
        out[slab] = (
            here + along * (lower + upper - twice) + across * (beneath + above - twice)
        )
        pltpu.make_async_copy(out.at[slab], out_hbm.at[slab], out_sem.at[slab]).start()

    for slab in range(slabs):
        pltpu.make_async_copy(out.at[slab], out_hbm.at[slab], out_sem.at[slab]).wait()
    drain(mass.at[pl.ds(0, n - 1)], mass_send)
    drain(total.at[pl.ds(0, m - 1)], total_send)
    drain(edge_in.at[pl.ds(0, n - 1)], edge_send)
    drain(halo_in.at[0], halo_send.at[0])
    drain(halo_in.at[1], halo_send.at[1])

    def wait_sent(chunk, _):
        drain(pieces(n - 1), send1.at[chunk])
        drain(pieces(n - 1), send2.at[chunk])
        return 0

    lax.fori_loop(0, chunks - 1, wait_sent, 0)
    wait_last(send1.at[chunks - 1])

    @pl.when(held)
    def _():
        drain(pieces(n - 1), send2.at[chunks - 1])


def shards(n, m, fields, shifts, area, gravity, kappa_az, kappa_rad):
    kinds, layers, rows, cols = fields.shape
    slabs = kinds * layers
    chunks = -(-(slabs * (rows // SUB)) // n)
    line = (1, rows)
    f32 = jnp.float32
    dma = pltpu.SemaphoreType.DMA
    vmem = pl.BlockSpec(memory_space=pltpu.VMEM)
    hbm = pl.BlockSpec(memory_space=pltpu.HBM)
    assert 2 * SUB * chunks <= LANES
    slab_pad = -(-slabs // SUB) * SUB
    updated, enclosed = pl.pallas_call(
        functools.partial(kernel, n, m, layers),
        out_shape=(
            jax.ShapeDtypeStruct((slabs, rows, cols), f32),
            jax.ShapeDtypeStruct(line, f32),
        ),
        in_specs=[hbm] * 6,
        out_specs=(hbm, vmem),
        scratch_shapes=[
            pltpu.VMEM((slabs, rows, cols), f32),
            dma((slabs,)),
            pltpu.VMEM((slabs, rows, cols), f32),
            pltpu.VMEM(line, jnp.int32),
            pltpu.VMEM(line, f32), pltpu.VMEM(line, f32), pltpu.VMEM(line, f32), pltpu.VMEM(line, f32),
            dma((6,)),
            pltpu.VMEM((chunks, n, SUB, cols), f32),
            pltpu.VMEM((chunks, n, SUB, cols), f32),
            pltpu.VMEM((slabs, rows, cols), f32),
            pltpu.VMEM((n, SUB, LANES), f32),
            pltpu.VMEM((n, 1, LANES), f32),
            pltpu.VMEM((n, 1, LANES), f32),
            pltpu.VMEM((n, 1, LANES), f32),
            pltpu.VMEM((m, 1, LANES), f32),
            pltpu.VMEM((rows, LANES), jnp.int32),
            pltpu.VMEM((4, slab_pad, cols), f32),
            dma((chunks,)), dma((chunks,)), dma((chunks,)), dma((chunks,)),
            dma, dma, dma, dma, dma, dma, dma((2,)), dma((2,)),
        ],
        compiler_params=pltpu.CompilerParams(
            collective_id=0, has_side_effects=True, vmem_limit_bytes=60 * 1024 * 1024
        ),
    )(
        fields.reshape(slabs, rows, cols), shifts.reshape(line), area.reshape(line),
        gravity.reshape(line), kappa_az.reshape(line), kappa_rad.reshape(line),
    )
    return updated.reshape(fields.shape), enclosed.reshape(rows)


def solution(mesh):
    placed = (P(None, None, "rad", "az"), P("rad"), P("rad"), P("rad"), P("rad"), P("rad"))
    return jax.shard_map(
        functools.partial(shards, mesh.shape["az"], mesh.shape["rad"]),
        mesh=mesh,
        in_specs=placed,
        out_specs=(P(None, None, "rad", "az"), P("rad")),
        check_vma=False,
    )
```

```python
import functools

import jax
import jax.numpy as jnp
from jax import lax
from jax.experimental import pallas as pl
from jax.experimental.pallas import tpu as pltpu
from jax.sharding import PartitionSpec as P

MESH = pl.DeviceIdType.MESH
SUB = 8
GROUP = 16
LANES = 128
star_mass = 1.0


def kernel(
    n, m, layers,
    source, shifts_in, area_in, gravity_in, kappa_az_in, kappa_rad_in,
    out_hbm, enclosed_out,
    out, out_sem, fields, shifts, area, gravity, kappa_az, kappa_rad, load_sem,
    win, wout, adv, edge_sum, edge_out, edge_in, mass, total, shift_table, halo_in,
    send1, recv1, send2, recv2, mass_send, mass_recv, total_send, total_recv,
    edge_send, edge_recv, halo_send, halo_recv,
):
    slabs, rows, cols = fields.shape
    per_slab = rows // GROUP
    groups = slabs * per_slab
    chunks = -(-groups // n)
    last = groups - n * (chunks - 1)
    me = lax.axis_index("az")
    ring = lax.axis_index("rad")

    def peer(step):
        return lax.rem(me + step, n)

    def far_peer(turn):
        odd = lax.rem(turn, 2)
        return peer(n // 2 + (lax.div(turn, 2) + odd) * (2 * odd - 1))

    def rad_peer(step):
        return lax.rem(ring + step, m)

    def place(group):
        slab = lax.rem(group, slabs)
        block = lax.rem(per_slab - lax.div(group, slabs), per_slab)
        return slab, pl.ds(pl.multiple_of(block * GROUP, GROUP), GROUP)

    def owner(index):
        if 4 * last == 3 * n:
            return index // 3 * 4 + (index % 3 + 1 + index // 3) % 4
        return (index * n + n - 1) // last

    def last_of(device):
        if 4 * last == 3 * n:
            four = lax.div(device, 4)
            spot = lax.rem(device + 3 + 3 * four, 4)
            return spot < 3, n * (chunks - 1) + 3 * four + spot
        index = lax.div(device * last, n)
        held = lax.div(index * n + n - 1, last) == device
        return held, n * (chunks - 1) + index

    def to_peer(src, dst, send, recv, device):
        return pltpu.make_async_remote_copy(
            src_ref=src, dst_ref=dst, send_sem=send, recv_sem=recv,
            device_id={"az": device}, device_id_type=MESH,
        )

    def to_rad(src, dst, send, recv, device):
        return pltpu.make_async_remote_copy(
            src_ref=src, dst_ref=dst, send_sem=send, recv_sem=recv,
            device_id={"rad": device}, device_id_type=MESH,
        )

    def drain(ref, sem):
        pltpu.make_async_copy(ref, ref, sem).wait()

    def pieces(count):
        return win.at[0, pl.ds(0, count)]

    loads = [
        pltpu.make_async_copy(here, there, load_sem.at[i])
        for i, (here, there) in enumerate((
            (source, fields), (shifts_in, shifts), (area_in, area),
            (gravity_in, gravity), (kappa_az_in, kappa_az), (kappa_rad_in, kappa_rad),
        ))
    ]
    for load in loads:
        load.start()

    barrier = pltpu.get_barrier_semaphore()

    def greet(step, _):
        pl.semaphore_signal(barrier, inc=1, device_id={"az": peer(step)}, device_id_type=MESH)
        return 0

    def greet_rad(step, _):
        pl.semaphore_signal(barrier, inc=1, device_id={"rad": rad_peer(step)}, device_id_type=MESH)
        return 0

    lax.fori_loop(1, n, greet, 0)
    lax.fori_loop(1, m, greet_rad, 0)

    row_at = lax.broadcasted_iota(jnp.int32, (rows, LANES), 0)
    lane_at = lax.broadcasted_iota(jnp.int32, (rows, LANES), 1)
    square_row = lax.broadcasted_iota(jnp.int32, (rows, rows), 0)
    square_lane = lax.broadcasted_iota(jnp.int32, (rows, rows), 1)

    def as_column(line):
        return jnp.sum(jnp.where(square_row == square_lane, line, 0.0), axis=1, keepdims=True)

    for load in loads:
        load.wait()
    density = fields[0]
    for z in range(1, layers):
        density = density + fields[z]
    local = jnp.sum(density, axis=1, keepdims=True)
    mass[me] = jnp.sum(jnp.where(row_at == lane_at, local, 0.0), axis=0, keepdims=True)

    pl.semaphore_wait(barrier, n - 1 + m - 1)

    def send_mass(step, _):
        to_peer(mass.at[me], mass.at[me], mass_send, mass_recv, peer(step)).start()
        return 0

    lax.fori_loop(1, n, send_mass, 0)

    def send_rows(chunk, _):
        def one(turn, _):
            device = far_peer(turn)
            slab, block = place(n * chunk + device)
            to_peer(
                source.at[slab, block], win.at[chunk, me], send1.at[chunk], recv1.at[chunk], device
            ).start()
            return 0

        return lax.fori_loop(0, n - 1, one, 0)

    lax.fori_loop(0, chunks - 1, send_rows, 0)

    def send_last(turn, _):
        device = far_peer(turn)
        held, group = last_of(device)

        @pl.when(held)
        def _():
            slab, block = place(group)
            to_peer(
                source.at[slab, block], win.at[chunks - 1, me],
                send1.at[chunks - 1], recv1.at[chunks - 1], device,
            ).start()

        return 0

    lax.fori_loop(0, n - 1, send_last, 0)

    shift_column = as_column(shifts[...].astype(jnp.float32)).astype(jnp.int32)
    shift_rows = jnp.broadcast_to(shift_column, (rows, LANES))
    shift_table[...] = shift_rows

    cells = n * cols
    spots = 2 * GROUP
    small = lax.broadcasted_iota(jnp.int32, (SUB, LANES), 1) - lax.broadcasted_iota(jnp.int32, (SUB, LANES), 0)

    def roll_chunk(chunk, group):
        slab, block = place(group)
        win[chunk, me] = fields[slab, block, :]
        amounts = shift_table[block, :]
        for part in range(0, GROUP, SUB):
            here = slice(part, part + SUB)
            amount = amounts[here, :1]
            row = jnp.concatenate([win[chunk, i, here] for i in range(n)], axis=1)
            for bit in range((cells - 1).bit_length()):
                rolled = pltpu.roll(row, 1 << bit, axis=1)
                row = jnp.where((amount >> bit) & 1 == 1, rolled, row)
            for i in range(n):
                wout[chunk, i, here] = row[:, i * cols:(i + 1) * cols]
                low = (i * cols - 1) % cells
                high = (i * cols + cols) % cells
                spot = spots * chunk + part
                edge_sum[i] = jnp.where(
                    small == spot, row[:, low:low + 1],
                    jnp.where(small == spot + GROUP, row[:, high:high + 1], edge_sum[i]),
                )
        adv[slab, block, :] = wout[chunk, me]

        def back(turn, _):
            device = far_peer(turn)
            to_peer(
                wout.at[chunk, device], adv.at[slab, block], send2.at[chunk], recv2.at[chunk], device
            ).start()
            return 0

        lax.fori_loop(0, n - 1, back, 0)
    edge_sum[...] = jnp.zeros(edge_sum.shape, jnp.float32)

    def turn(chunk, _):
        drain(pieces(n - 1), recv1.at[chunk])
        roll_chunk(chunk, n * chunk + me)
        return 0

    lax.fori_loop(0, chunks - 1, turn, 0)
    held, group = last_of(me)

    @pl.when(held)
    def _():
        drain(pieces(n - 1), recv1.at[chunks - 1])
        roll_chunk(chunks - 1, group)

    edge_out[...] = jnp.sum(edge_sum[...], axis=1, keepdims=True)
    edge_in[me] = edge_out[me]

    def send_edges(step, _):
        device = peer(step)
        to_peer(edge_out.at[device], edge_in.at[me], edge_send, edge_recv, device).start()
        return 0

    lax.fori_loop(1, n, send_edges, 0)

    def wait_back(chunk, _):
        drain(pieces(n - 1), recv2.at[chunk])
        return 0

    def wait_last(sem):
        @pl.when(held)
        def _():
            drain(pieces(last - 1), sem)

        @pl.when(jnp.logical_not(held))
        def _():
            drain(pieces(last), sem)

    drain(mass.at[pl.ds(0, n - 1)], mass_recv)
    cycle_mass = jnp.sum(mass[...], axis=0)[:, :rows]
    row_mass = area[...] * cycle_mass / (2.0 * (n * cols))
    block_mass = jnp.sum(row_mass, axis=1, keepdims=True)
    total[ring] = jnp.broadcast_to(block_mass, (1, LANES))

    def send_total(step, _):
        to_rad(total.at[ring], total.at[ring], total_send, total_recv, rad_peer(step)).start()
        return 0

    lax.fori_loop(1, m, send_total, 0)
    before = jnp.sum(jnp.where(square_lane < square_row, row_mass, 0.0), axis=1, keepdims=True)
    own = as_column(row_mass)
    drain(total.at[pl.ds(0, m - 1)], total_recv)
    rank = lax.broadcasted_iota(jnp.int32, (m, 1, LANES), 0)
    offset = jnp.sum(jnp.where(rank < ring, total[...], 0.0), axis=0)[:, :1]
    enclosed = star_mass + offset + before + 0.5 * own
    enclosed_out[...] = jnp.sum(jnp.where(square_row == square_lane, enclosed, 0.0), axis=0, keepdims=True)
    pull = as_column(gravity[...]) * enclosed

    early = (2 * slabs - 1) // n + 1
    lax.fori_loop(0, min(early, chunks - 1), wait_back, 0)
    if early == chunks:
        wait_last(recv2.at[chunks - 1])

    for side, at in ((1, 0), (2, rows - 1)):
        rate = pull[at:at + 1, :]
        for slab in range(slabs):
            line = adv[slab, at:at + 1, :]
            if slab // layers in (1, 3):
                below = slab - layers if slab // layers == 1 else slab - 2 * layers
                line = line - rate * adv[below, at:at + 1, :]
            halo_in[side - 1, slab:slab + 1, :] = line
    to_rad(halo_in.at[0], halo_in.at[2], halo_send.at[0], halo_recv.at[0], rad_peer(m - 1)).start()
    to_rad(halo_in.at[1], halo_in.at[3], halo_send.at[1], halo_recv.at[1], rad_peer(1)).start()

    if early < chunks:
        lax.fori_loop(early, chunks - 1, wait_back, 0)
        wait_last(recv2.at[chunks - 1])
    drain(edge_in.at[pl.ds(0, n - 1)], edge_recv)
    drain(halo_in.at[0], halo_recv.at[0])
    drain(halo_in.at[1], halo_recv.at[1])

    along = as_column(kappa_az[...])
    across = as_column(kappa_rad[...])
    wide_row = lax.broadcasted_iota(jnp.int32, (rows, cols), 0)
    wide_lane = lax.broadcasted_iota(jnp.int32, (rows, cols), 1)
    inner = ring > 0
    outer = ring < m - 1

    def ends(slab):
        sides = ([], [])
        for block in range(per_slab):
            index = ((per_slab - block) % per_slab) * slabs + slab
            chunk = index // n
            device = index % n if chunk < chunks - 1 else owner(index - n * chunk)
            line = edge_in[device]
            for side in range(2):
                for part in range(0, GROUP, SUB):
                    spot = jnp.where(small == spots * chunk + GROUP * side + part, line, 0.0)
                    sides[side].append(jnp.sum(spot, axis=1, keepdims=True))
        return jnp.concatenate(sides[0], axis=0), jnp.concatenate(sides[1], axis=0)

    edges = [ends(slab) for slab in range(slabs)]
    for slab in range(slabs):
        here = adv[slab]
        left, right = edges[slab]
        if slab // layers in (1, 3):
            below = slab - layers if slab // layers == 1 else slab - 2 * layers
            here = here - pull * adv[below]
            other_left, other_right = edges[below]
            left = left - pull * other_left
            right = right - pull * other_right
        top = jnp.where(inner, halo_in[3, slab:slab + 1, :], 0.0)
        bottom = jnp.where(outer, halo_in[2, slab:slab + 1, :], 0.0)
        lower = jnp.where(wide_lane == 0, left, pltpu.roll(here, 1, axis=1))
        upper = jnp.where(wide_lane == cols - 1, right, pltpu.roll(here, cols - 1, axis=1))
        above = jnp.where(wide_row == 0, top, pltpu.roll(here, 1, axis=0))
        beneath = jnp.where(wide_row == rows - 1, bottom, pltpu.roll(here, rows - 1, axis=0))
        twice = 2.0 * here
        out[slab] = (
            here + along * (lower + upper - twice) + across * (beneath + above - twice)
        )
        pltpu.make_async_copy(out.at[slab], out_hbm.at[slab], out_sem.at[slab]).start()

    for slab in range(slabs):
        pltpu.make_async_copy(out.at[slab], out_hbm.at[slab], out_sem.at[slab]).wait()
    drain(mass.at[pl.ds(0, n - 1)], mass_send)
    drain(total.at[pl.ds(0, m - 1)], total_send)
    drain(edge_in.at[pl.ds(0, n - 1)], edge_send)
    drain(halo_in.at[0], halo_send.at[0])
    drain(halo_in.at[1], halo_send.at[1])

    def wait_sent(chunk, _):
        drain(pieces(n - 1), send1.at[chunk])
        drain(pieces(n - 1), send2.at[chunk])
        return 0

    lax.fori_loop(0, chunks - 1, wait_sent, 0)
    wait_last(send1.at[chunks - 1])

    @pl.when(held)
    def _():
        drain(pieces(n - 1), send2.at[chunks - 1])


def shards(n, m, fields, shifts, area, gravity, kappa_az, kappa_rad):
    kinds, layers, rows, cols = fields.shape
    slabs = kinds * layers
    chunks = -(-(slabs * (rows // GROUP)) // n)
    line = (1, rows)
    f32 = jnp.float32
    dma = pltpu.SemaphoreType.DMA
    vmem = pl.BlockSpec(memory_space=pltpu.VMEM)
    hbm = pl.BlockSpec(memory_space=pltpu.HBM)
    assert 2 * GROUP * chunks <= LANES
    slab_pad = -(-slabs // SUB) * SUB
    updated, enclosed = pl.pallas_call(
        functools.partial(kernel, n, m, layers),
        out_shape=(
            jax.ShapeDtypeStruct((slabs, rows, cols), f32),
            jax.ShapeDtypeStruct(line, f32),
        ),
        in_specs=[hbm] * 6,
        out_specs=(hbm, vmem),
        scratch_shapes=[
            pltpu.VMEM((slabs, rows, cols), f32),
            dma((slabs,)),
            pltpu.VMEM((slabs, rows, cols), f32),
            pltpu.VMEM(line, jnp.int32),
            pltpu.VMEM(line, f32), pltpu.VMEM(line, f32), pltpu.VMEM(line, f32), pltpu.VMEM(line, f32),
            dma((6,)),
            pltpu.VMEM((chunks, n, GROUP, cols), f32),
            pltpu.VMEM((chunks, n, GROUP, cols), f32),
            pltpu.VMEM((slabs, rows, cols), f32),
            pltpu.VMEM((n, SUB, LANES), f32),
            pltpu.VMEM((n, 1, LANES), f32),
            pltpu.VMEM((n, 1, LANES), f32),
            pltpu.VMEM((n, 1, LANES), f32),
            pltpu.VMEM((m, 1, LANES), f32),
            pltpu.VMEM((rows, LANES), jnp.int32),
            pltpu.VMEM((4, slab_pad, cols), f32),
            dma((chunks,)), dma((chunks,)), dma((chunks,)), dma((chunks,)),
            dma, dma, dma, dma, dma, dma, dma((2,)), dma((2,)),
        ],
        compiler_params=pltpu.CompilerParams(
            collective_id=0, has_side_effects=True, vmem_limit_bytes=60 * 1024 * 1024
        ),
    )(
        fields.reshape(slabs, rows, cols), shifts.reshape(line), area.reshape(line),
        gravity.reshape(line), kappa_az.reshape(line), kappa_rad.reshape(line),
    )
    return updated.reshape(fields.shape), enclosed.reshape(rows)


def solution(mesh):
    placed = (P(None, None, "rad", "az"), P("rad"), P("rad"), P("rad"), P("rad"), P("rad"))
    return jax.shard_map(
        functools.partial(shards, mesh.shape["az"], mesh.shape["rad"]),
        mesh=mesh,
        in_specs=placed,
        out_specs=(P(None, None, "rad", "az"), P("rad")),
        check_vma=False,
    )
```

```python
import functools

import jax
import jax.numpy as jnp
from jax import lax
from jax.experimental import pallas as pl
from jax.experimental.pallas import tpu as pltpu
from jax.sharding import PartitionSpec as P

MESH = pl.DeviceIdType.MESH
SUB = 8
GROUP = 8
LANES = 128
star_mass = 1.0


def owner(n, last, index):
    if n == 2 * last:
        return 2 * index + (index // 2 + index) % 2
    return (index * n + n - 1) // last


def source_of(slab, layers):
    return slab - {1: layers, 3: 2 * layers}.get(slab // layers, 0)


def exchange(
    n, m, layers,
    source, shifts_in, area_in, gravity_in,
    adv, edge_in, halo_in, enclosed_out,
    fields, shifts, area, gravity, load_sem,
    win, wout, edge_sum, edge_out, mass, total, shift_table, border, halo_out,
    own_sem, border_sem,
    send1, recv1, send2, recv2, mass_send, mass_recv, total_send, total_recv,
    edge_send, edge_recv, halo_send, halo_recv,
):
    slabs, rows, cols = fields.shape
    per_slab = rows // GROUP
    groups = slabs * per_slab
    chunks = -(-groups // n)
    last = groups - n * (chunks - 1)
    me = lax.axis_index("az")
    ring = lax.axis_index("rad")

    def peer(step):
        return lax.rem(me + step, n)

    def far_peer(turn):
        odd = lax.rem(turn, 2)
        return peer(n // 2 + (lax.div(turn, 2) + odd) * (2 * odd - 1))

    def rad_peer(step):
        return lax.rem(ring + step, m)

    def place(group):
        slab = lax.rem(group, slabs)
        block = lax.rem(per_slab - lax.div(group, slabs), per_slab)
        return slab, pl.ds(pl.multiple_of(block * GROUP, GROUP), GROUP)

    def last_of(device):
        index = lax.div(device * last, n)
        return owner(n, last, index) == device, n * (chunks - 1) + index

    def to_peer(src, dst, send, recv, device):
        return pltpu.make_async_remote_copy(
            src_ref=src, dst_ref=dst, send_sem=send, recv_sem=recv,
            device_id={"az": device}, device_id_type=MESH,
        )

    def to_rad(src, dst, send, recv, device):
        return pltpu.make_async_remote_copy(
            src_ref=src, dst_ref=dst, send_sem=send, recv_sem=recv,
            device_id={"rad": device}, device_id_type=MESH,
        )

    def drain(ref, sem):
        pltpu.make_async_copy(ref, ref, sem).wait()

    def pieces(count):
        return win.at[0, pl.ds(0, count)]

    loads = [
        pltpu.make_async_copy(here, there, load_sem.at[i])
        for i, (here, there) in enumerate((
            (source, fields), (shifts_in, shifts), (area_in, area),
            (gravity_in, gravity),
        ))
    ]
    for load in loads:
        load.start()

    barrier = pltpu.get_barrier_semaphore()

    def greet(step, _):
        pl.semaphore_signal(barrier, inc=1, device_id={"az": peer(step)}, device_id_type=MESH)
        return 0

    def greet_rad(step, _):
        pl.semaphore_signal(barrier, inc=1, device_id={"rad": rad_peer(step)}, device_id_type=MESH)
        return 0

    lax.fori_loop(1, n, greet, 0)
    lax.fori_loop(1, m, greet_rad, 0)

    row_at = lax.broadcasted_iota(jnp.int32, (rows, LANES), 0)
    lane_at = lax.broadcasted_iota(jnp.int32, (rows, LANES), 1)
    square_row = lax.broadcasted_iota(jnp.int32, (rows, rows), 0)
    square_lane = lax.broadcasted_iota(jnp.int32, (rows, rows), 1)

    def as_column(line):
        return jnp.sum(jnp.where(square_row == square_lane, line, 0.0), axis=1, keepdims=True)

    for load in loads:
        load.wait()
    density = fields[0]
    for z in range(1, layers):
        density = density + fields[z]
    local = jnp.sum(density, axis=1, keepdims=True)
    mass[me] = jnp.sum(jnp.where(row_at == lane_at, local, 0.0), axis=0, keepdims=True)

    pl.semaphore_wait(barrier, n - 1 + m - 1)

    def send_mass(step, _):
        to_peer(mass.at[me], mass.at[me], mass_send, mass_recv, peer(step)).start()
        return 0

    lax.fori_loop(1, n, send_mass, 0)

    def send_rows(chunk, _):
        def one(turn, _):
            device = far_peer(turn)
            slab, block = place(n * chunk + device)
            to_peer(
                source.at[slab, block], win.at[chunk, me], send1.at[chunk], recv1.at[chunk], device
            ).start()
            return 0

        return lax.fori_loop(0, n - 1, one, 0)

    lax.fori_loop(0, chunks - 1, send_rows, 0)

    def send_last(turn, _):
        device = far_peer(turn)
        held, group = last_of(device)

        @pl.when(held)
        def _():
            slab, block = place(group)
            to_peer(
                source.at[slab, block], win.at[chunks - 1, me],
                send1.at[chunks - 1], recv1.at[chunks - 1], device,
            ).start()

        return 0

    lax.fori_loop(0, n - 1, send_last, 0)

    shift_column = as_column(shifts[...].astype(jnp.float32)).astype(jnp.int32)
    shift_rows = jnp.broadcast_to(shift_column, (rows, LANES))
    shift_table[...] = shift_rows

    cells = n * cols
    spots = 2 * GROUP
    small = lax.broadcasted_iota(jnp.int32, (SUB, LANES), 1) - lax.broadcasted_iota(jnp.int32, (SUB, LANES), 0)

    def roll_chunk(chunk, group):
        slab, block = place(group)
        win[chunk, me] = fields[slab, block, :]
        amounts = shift_table[block, :]
        for part in range(0, GROUP, SUB):
            here = slice(part, part + SUB)
            amount = amounts[here, :1]
            row = jnp.concatenate([win[chunk, i, here] for i in range(n)], axis=1)
            for bit in range((cells - 1).bit_length()):
                rolled = pltpu.roll(row, 1 << bit, axis=1)
                row = jnp.where((amount >> bit) & 1 == 1, rolled, row)
            for i in range(n):
                wout[chunk, i, here] = row[:, i * cols:(i + 1) * cols]
                low = (i * cols - 1) % cells
                high = (i * cols + cols) % cells
                spot = spots * chunk + part
                edge_sum[i] = jnp.where(
                    small == spot, row[:, low:low + 1],
                    jnp.where(small == spot + GROUP, row[:, high:high + 1], edge_sum[i]),
                )
        pltpu.make_async_copy(wout.at[chunk, me], adv.at[slab, block], own_sem.at[chunk]).start()

        def back(turn, _):
            device = far_peer(turn)
            to_peer(
                wout.at[chunk, device], adv.at[slab, block], send2.at[chunk], recv2.at[chunk], device
            ).start()
            return 0

        lax.fori_loop(0, n - 1, back, 0)
    edge_sum[...] = jnp.zeros(edge_sum.shape, jnp.float32)

    def turn(chunk, _):
        drain(pieces(n - 1), recv1.at[chunk])
        roll_chunk(chunk, n * chunk + me)
        return 0

    lax.fori_loop(0, chunks - 1, turn, 0)
    held, group = last_of(me)

    @pl.when(held)
    def _():
        drain(pieces(n - 1), recv1.at[chunks - 1])
        roll_chunk(chunks - 1, group)

    edge_out[...] = jnp.sum(edge_sum[...], axis=1, keepdims=True)
    own_edges = pltpu.make_async_copy(edge_out.at[me], edge_in.at[me], border_sem.at[2])
    own_edges.start()

    def send_edges(step, _):
        device = peer(step)
        to_peer(edge_out.at[device], edge_in.at[me], edge_send, edge_recv, device).start()
        return 0

    lax.fori_loop(1, n, send_edges, 0)

    def wait_back(chunk, _):
        drain(pieces(n - 1), recv2.at[chunk])
        drain(wout.at[0, 0], own_sem.at[chunk])
        return 0

    def wait_last(sem, own):
        @pl.when(held)
        def _():
            drain(pieces(last - 1), sem)
            if own:
                drain(wout.at[0, 0], own_sem.at[chunks - 1])

        @pl.when(jnp.logical_not(held))
        def _():
            drain(pieces(last), sem)

    drain(mass.at[pl.ds(0, n - 1)], mass_recv)
    cycle_mass = jnp.sum(mass[...], axis=0)[:, :rows]
    row_mass = area[...] * cycle_mass / (2.0 * (n * cols))
    block_mass = jnp.sum(row_mass, axis=1, keepdims=True)
    total[ring] = jnp.broadcast_to(block_mass, (1, LANES))

    def send_total(step, _):
        to_rad(total.at[ring], total.at[ring], total_send, total_recv, rad_peer(step)).start()
        return 0

    lax.fori_loop(1, m, send_total, 0)
    before = jnp.sum(jnp.where(square_lane < square_row, row_mass, 0.0), axis=1, keepdims=True)
    own = as_column(row_mass)
    drain(total.at[pl.ds(0, m - 1)], total_recv)
    rank = lax.broadcasted_iota(jnp.int32, (m, 1, LANES), 0)
    offset = jnp.sum(jnp.where(rank < ring, total[...], 0.0), axis=0)[:, :1]
    enclosed = star_mass + offset + before + 0.5 * own
    enclosed_out[...] = jnp.sum(jnp.where(square_row == square_lane, enclosed, 0.0), axis=0, keepdims=True)
    pull = as_column(gravity[...]) * enclosed

    early = (2 * slabs - 1) // n + 1
    lax.fori_loop(0, min(early, chunks - 1), wait_back, 0)
    if early == chunks:
        wait_last(recv2.at[chunks - 1], True)

    rims = [
        pltpu.make_async_copy(adv.at[:, pl.ds(at, SUB)], border.at[side], border_sem.at[side])
        for side, at in enumerate((0, rows - SUB))
    ]
    for rim in rims:
        rim.start()
    for rim in rims:
        rim.wait()
    for side, at, row in ((0, 0, 0), (1, rows - 1, SUB - 1)):
        rate = pull[at:at + 1, :]
        for slab in range(slabs):
            line = border[side, slab, row:row + 1, :]
            below = source_of(slab, layers)
            if below != slab:
                line = line - rate * border[side, below, row:row + 1, :]
            halo_out[side, slab:slab + 1, :] = line
    to_rad(halo_out.at[0], halo_in.at[1], halo_send.at[0], halo_recv.at[0], rad_peer(m - 1)).start()
    to_rad(halo_out.at[1], halo_in.at[0], halo_send.at[1], halo_recv.at[1], rad_peer(1)).start()

    if early < chunks:
        lax.fori_loop(early, chunks - 1, wait_back, 0)
        wait_last(recv2.at[chunks - 1], True)
    drain(edge_out.at[pl.ds(0, n - 1)], edge_recv)
    drain(halo_out.at[0], halo_recv.at[0])
    drain(halo_out.at[1], halo_recv.at[1])
    own_edges.wait()

    drain(mass.at[pl.ds(0, n - 1)], mass_send)
    drain(total.at[pl.ds(0, m - 1)], total_send)
    drain(edge_out.at[pl.ds(0, n - 1)], edge_send)
    drain(halo_out.at[0], halo_send.at[0])
    drain(halo_out.at[1], halo_send.at[1])

    def wait_sent(chunk, _):
        drain(pieces(n - 1), send1.at[chunk])
        drain(pieces(n - 1), send2.at[chunk])
        return 0

    lax.fori_loop(0, chunks - 1, wait_sent, 0)
    wait_last(send1.at[chunks - 1], False)

    @pl.when(held)
    def _():
        drain(pieces(n - 1), send2.at[chunks - 1])

def diffuse(
    n, m, layers,
    adv_in, edge_in, halo_in, enclosed_in, gravity_in, kappa_az_in, kappa_rad_in,
    out_hbm, enclosed_out,
    adv, edge_lines, halo, enclosed, gravity, kappa_az, kappa_rad, out, adv_sem, load_sem, out_sem,
):
    slabs, rows, cols = adv.shape
    per_slab = rows // GROUP
    groups = slabs * per_slab
    chunks = -(-groups // n)
    last = groups - n * (chunks - 1)
    ring = lax.axis_index("rad")

    loads = [
        pltpu.make_async_copy(here, there, load_sem.at[i])
        for i, (here, there) in enumerate((
            (edge_in, edge_lines), (halo_in, halo), (enclosed_in, enclosed),
            (gravity_in, gravity), (kappa_az_in, kappa_az), (kappa_rad_in, kappa_rad),
        ))
    ]
    slab_loads = [
        pltpu.make_async_copy(adv_in.at[slab], adv.at[slab], adv_sem.at[slab]) for slab in range(slabs)
    ]
    for load in loads + slab_loads:
        load.start()

    square_row = lax.broadcasted_iota(jnp.int32, (rows, rows), 0)
    square_lane = lax.broadcasted_iota(jnp.int32, (rows, rows), 1)

    def as_column(line):
        return jnp.sum(jnp.where(square_row == square_lane, line, 0.0), axis=1, keepdims=True)

    spots = 2 * GROUP
    small = lax.broadcasted_iota(jnp.int32, (SUB, LANES), 1) - lax.broadcasted_iota(jnp.int32, (SUB, LANES), 0)
    for load in loads:
        load.wait()
    enclosed_out[...] = enclosed[...]
    pull = as_column(gravity[...]) * as_column(enclosed[...])
    along = as_column(kappa_az[...])
    across = as_column(kappa_rad[...])
    wide_row = lax.broadcasted_iota(jnp.int32, (rows, cols), 0)
    wide_lane = lax.broadcasted_iota(jnp.int32, (rows, cols), 1)
    inner = ring > 0
    outer = ring < m - 1

    def ends(slab):
        sides = ([], [])
        for block in range(per_slab):
            index = ((per_slab - block) % per_slab) * slabs + slab
            chunk = index // n
            device = index % n if chunk < chunks - 1 else owner(n, last, index - n * chunk)
            line = edge_lines[device]
            for side in range(2):
                for part in range(0, GROUP, SUB):
                    spot = jnp.where(small == spots * chunk + GROUP * side + part, line, 0.0)
                    sides[side].append(jnp.sum(spot, axis=1, keepdims=True))
        return jnp.concatenate(sides[0], axis=0), jnp.concatenate(sides[1], axis=0)

    edges = [ends(slab) for slab in range(slabs)]
    for slab in range(slabs):
        slab_loads[slab].wait()
        here = adv[slab]
        left, right = edges[slab]
        below = source_of(slab, layers)
        if below != slab:
            here = here - pull * adv[below]
            other_left, other_right = edges[below]
            left = left - pull * other_left
            right = right - pull * other_right
        top = jnp.where(inner, halo[0, slab:slab + 1, :], 0.0)
        bottom = jnp.where(outer, halo[1, slab:slab + 1, :], 0.0)
        lower = jnp.where(wide_lane == 0, left, pltpu.roll(here, 1, axis=1))
        upper = jnp.where(wide_lane == cols - 1, right, pltpu.roll(here, cols - 1, axis=1))
        above = jnp.where(wide_row == 0, top, pltpu.roll(here, 1, axis=0))
        beneath = jnp.where(wide_row == rows - 1, bottom, pltpu.roll(here, rows - 1, axis=0))
        twice = 2.0 * here
        out[slab] = (
            here + along * (lower + upper - twice) + across * (beneath + above - twice)
        )
        pltpu.make_async_copy(out.at[slab], out_hbm.at[slab], out_sem.at[slab]).start()

    for slab in range(slabs):
        pltpu.make_async_copy(out.at[slab], out_hbm.at[slab], out_sem.at[slab]).wait()


def shards(n, m, fields, shifts, area, gravity, kappa_az, kappa_rad):
    kinds, layers, rows, cols = fields.shape
    slabs = kinds * layers
    chunks = -(-(slabs * (rows // GROUP)) // n)
    line = (1, rows)
    f32 = jnp.float32
    dma = pltpu.SemaphoreType.DMA
    vmem = pl.BlockSpec(memory_space=pltpu.VMEM)
    hbm = pl.BlockSpec(memory_space=pltpu.HBM)
    assert 2 * GROUP * chunks <= LANES
    slab_pad = -(-slabs // SUB) * SUB
    whole = jax.ShapeDtypeStruct((slabs, rows, cols), f32)
    params = pltpu.CompilerParams(vmem_limit_bytes=60 * 1024 * 1024)
    one = jax.ShapeDtypeStruct(line, f32)
    shifts, area, gravity, kappa_az, kappa_rad = (
        value.reshape(line) for value in (shifts, area, gravity, kappa_az, kappa_rad)
    )
    adv, edges, halo, enclosed = pl.pallas_call(
        functools.partial(exchange, n, m, layers),
        out_shape=(
            whole,
            jax.ShapeDtypeStruct((n, 1, LANES), f32),
            jax.ShapeDtypeStruct((2, slab_pad, cols), f32),
            one,
        ),
        in_specs=[hbm] * 4,
        out_specs=(hbm, hbm, hbm, vmem),
        scratch_shapes=[
            pltpu.VMEM((slabs, rows, cols), f32),
            pltpu.VMEM(line, jnp.int32), pltpu.VMEM(line, f32), pltpu.VMEM(line, f32),
            dma((4,)),
            pltpu.VMEM((chunks, n, GROUP, cols), f32),
            pltpu.VMEM((chunks, n, GROUP, cols), f32),
            pltpu.VMEM((n, SUB, LANES), f32),
            pltpu.VMEM((n, 1, LANES), f32),
            pltpu.VMEM((n, 1, LANES), f32),
            pltpu.VMEM((m, 1, LANES), f32),
            pltpu.VMEM((rows, LANES), jnp.int32),
            pltpu.VMEM((2, slabs, SUB, cols), f32),
            pltpu.VMEM((2, slab_pad, cols), f32),
            dma((chunks,)), dma((3,)),
            dma((chunks,)), dma((chunks,)), dma((chunks,)), dma((chunks,)),
            dma, dma, dma, dma, dma, dma, dma((2,)), dma((2,)),
        ],
        compiler_params=pltpu.CompilerParams(
            collective_id=0, has_side_effects=True, vmem_limit_bytes=60 * 1024 * 1024
        ),
    )(fields.reshape(slabs, rows, cols), shifts, area, gravity)
    updated, enclosed = pl.pallas_call(
        functools.partial(diffuse, n, m, layers),
        out_shape=(whole, one),
        in_specs=[hbm] * 7,
        out_specs=(hbm, vmem),
        scratch_shapes=[
            pltpu.VMEM((slabs, rows, cols), f32),
            pltpu.VMEM((n, 1, LANES), f32),
            pltpu.VMEM((2, slab_pad, cols), f32),
            pltpu.VMEM(line, f32), pltpu.VMEM(line, f32), pltpu.VMEM(line, f32), pltpu.VMEM(line, f32),
            pltpu.VMEM((slabs, rows, cols), f32),
            dma((slabs,)), dma((6,)), dma((slabs,)),
        ],
        compiler_params=params,
    )(adv, edges, halo, enclosed, gravity, kappa_az, kappa_rad)
    return updated.reshape(fields.shape), enclosed.reshape(rows)


def solution(mesh):
    placed = (P(None, None, "rad", "az"), P("rad"), P("rad"), P("rad"), P("rad"), P("rad"))
    return jax.shard_map(
        functools.partial(shards, mesh.shape["az"], mesh.shape["rad"]),
        mesh=mesh,
        in_specs=placed,
        out_specs=(P(None, None, "rad", "az"), P("rad")),
        check_vma=False,
    )
```

```python
import functools

import jax
import jax.numpy as jnp
from jax import lax
from jax.experimental import pallas as pl
from jax.experimental.pallas import tpu as pltpu
from jax.sharding import PartitionSpec as P

MESH = pl.DeviceIdType.MESH
SUB = 8
LANES = 128
star_mass = 1.0


def kernel(
    n, m, layers,
    source, shifts_in, area_in, gravity_in, kappa_az_in, kappa_rad_in,
    out, enclosed_out,
    fields, shifts, area, gravity, kappa_az, kappa_rad, load_sem,
    win, wout, adv, edge_out, edge_in, mass, total, shift_table, tables, halo_in,
    send1, recv1, send2, recv2, mass_send, mass_recv, total_send, total_recv,
    edge_send, edge_recv, halo_send, halo_recv,
):
    slabs, rows, cols = fields.shape
    per_slab = rows // SUB
    groups = slabs * per_slab
    chunks = -(-groups // n)
    last = groups - n * (chunks - 1)
    me = lax.axis_index("az")
    ring = lax.axis_index("rad")

    def peer(step):
        return lax.rem(me + step, n)

    def rad_peer(step):
        return lax.rem(ring + step, m)

    def place(group):
        slab = lax.rem(group, slabs)
        block = lax.rem(per_slab - lax.div(group, slabs), per_slab)
        return slab, pl.ds(pl.multiple_of(block * SUB, SUB), SUB)

    def owner(index):
        if n == 2 * last:
            return 2 * index + lax.rem(lax.div(index, 2) + index, 2)
        return lax.div(index * n + n - 1, last)

    def last_of(device):
        index = lax.div(device * last, n)
        held = owner(index) == device
        return held, n * (chunks - 1) + index

    def to_peer(src, dst, send, recv, device):
        return pltpu.make_async_remote_copy(
            src_ref=src, dst_ref=dst, send_sem=send, recv_sem=recv,
            device_id={"az": device}, device_id_type=MESH,
        )

    def to_rad(src, dst, send, recv, device):
        return pltpu.make_async_remote_copy(
            src_ref=src, dst_ref=dst, send_sem=send, recv_sem=recv,
            device_id={"rad": device}, device_id_type=MESH,
        )

    def drain(ref, sem):
        pltpu.make_async_copy(ref, ref, sem).wait()

    def pieces(count):
        return win.at[0, pl.ds(0, count)]

    loads = [
        pltpu.make_async_copy(here, there, load_sem.at[i])
        for i, (here, there) in enumerate((
            (source, fields), (shifts_in, shifts), (area_in, area),
            (gravity_in, gravity), (kappa_az_in, kappa_az), (kappa_rad_in, kappa_rad),
        ))
    ]
    for load in loads:
        load.start()

    barrier = pltpu.get_barrier_semaphore()

    def greet(step, _):
        pl.semaphore_signal(barrier, inc=1, device_id={"az": peer(step)}, device_id_type=MESH)
        return 0

    def greet_rad(step, _):
        pl.semaphore_signal(barrier, inc=1, device_id={"rad": rad_peer(step)}, device_id_type=MESH)
        return 0

    lax.fori_loop(1, n, greet, 0)
    lax.fori_loop(1, m, greet_rad, 0)

    row_at = lax.broadcasted_iota(jnp.int32, (rows, LANES), 0)
    lane_at = lax.broadcasted_iota(jnp.int32, (rows, LANES), 1)
    square_row = lax.broadcasted_iota(jnp.int32, (rows, rows), 0)
    square_lane = lax.broadcasted_iota(jnp.int32, (rows, rows), 1)

    def as_column(line):
        return jnp.sum(jnp.where(square_row == square_lane, line, 0.0), axis=1, keepdims=True)

    for load in loads:
        load.wait()
    density = fields[0]
    for z in range(1, layers):
        density = density + fields[z]
    local = jnp.sum(density, axis=1, keepdims=True)
    mass[me] = jnp.sum(jnp.where(row_at == lane_at, local, 0.0), axis=0, keepdims=True)

    pl.semaphore_wait(barrier, n - 1 + m - 1)

    def send_mass(step, _):
        to_peer(mass.at[me], mass.at[me], mass_send, mass_recv, peer(step)).start()
        return 0

    lax.fori_loop(1, n, send_mass, 0)

    def send_rows(chunk, _):
        def one(step, _):
            device = peer(step)
            slab, block = place(n * chunk + device)
            to_peer(
                source.at[slab, block], win.at[chunk, me], send1.at[chunk], recv1.at[chunk], device
            ).start()
            return 0

        return lax.fori_loop(1, n, one, 0)

    lax.fori_loop(0, chunks - 1, send_rows, 0)

    def send_last(step, _):
        device = peer(step)
        held, group = last_of(device)

        @pl.when(held)
        def _():
            slab, block = place(group)
            to_peer(
                source.at[slab, block], win.at[chunks - 1, me],
                send1.at[chunks - 1], recv1.at[chunks - 1], device,
            ).start()

        return 0

    lax.fori_loop(1, n, send_last, 0)

    shift_column = as_column(shifts[...].astype(jnp.float32)).astype(jnp.int32)
    shift_rows = jnp.broadcast_to(shift_column, (rows, LANES))
    shift_table[...] = shift_rows

    cells = n * cols
    small = lax.broadcasted_iota(jnp.int32, (SUB, LANES), 1) - lax.broadcasted_iota(jnp.int32, (SUB, LANES), 0)

    def roll_chunk(chunk, group):
        slab, block = place(group)
        win[chunk, me] = fields[slab, block, :]
        amount = shift_table[block, :]
        amount = amount[:, :1]
        row = jnp.concatenate([win[chunk, i] for i in range(n)], axis=1)
        for bit in range((cells - 1).bit_length()):
            rolled = pltpu.roll(row, 1 << bit, axis=1)
            row = jnp.where((amount >> bit) & 1 == 1, rolled, row)
        for i in range(n):
            wout[chunk, i] = row[:, i * cols:(i + 1) * cols]
        adv[slab, block, :] = wout[chunk, me]

        def back(step, _):
            device = peer(step)
            to_peer(
                wout.at[chunk, device], adv.at[slab, block], send2.at[chunk], recv2.at[chunk], device
            ).start()
            return 0

        lax.fori_loop(1, n, back, 0)
        for i in range(n):
            low = (i * cols - 1) % cells
            high = (i * cols + cols) % cells
            ends = jnp.where(
                small == 0, row[:, low:low + 1],
                jnp.where(small == SUB, row[:, high:high + 1], 0.0),
            )
            edge_out[chunk, i] = jnp.sum(ends, axis=0, keepdims=True)
        edge_in[chunk, me] = edge_out[chunk, me]

        def back_edges(step, _):
            device = peer(step)
            to_peer(
                edge_out.at[chunk, device], edge_in.at[chunk, me],
                edge_send.at[chunk], edge_recv.at[chunk], device,
            ).start()
            return 0

        lax.fori_loop(1, n, back_edges, 0)

    def turn(chunk, _):
        drain(pieces(n - 1), recv1.at[chunk])
        roll_chunk(chunk, n * chunk + me)
        return 0

    lax.fori_loop(0, chunks - 1, turn, 0)
    held, group = last_of(me)

    @pl.when(held)
    def _():
        drain(pieces(n - 1), recv1.at[chunks - 1])
        roll_chunk(chunks - 1, group)

    def lines(count):
        return edge_in.at[0, pl.ds(0, count)]

    def wait_last(some, sem):
        @pl.when(held)
        def _():
            drain(some(last - 1), sem)

        @pl.when(jnp.logical_not(held))
        def _():
            drain(some(last), sem)

    drain(mass.at[pl.ds(0, n - 1)], mass_recv)
    cycle_mass = jnp.sum(mass[...], axis=0)[:, :rows]
    row_mass = area[...] * cycle_mass / (2.0 * (n * cols))
    block_mass = jnp.sum(row_mass, axis=1, keepdims=True)
    total[ring] = jnp.broadcast_to(block_mass, (1, LANES))

    def send_total(step, _):
        to_rad(total.at[ring], total.at[ring], total_send, total_recv, rad_peer(step)).start()
        return 0

    lax.fori_loop(1, m, send_total, 0)
    before = jnp.sum(jnp.where(square_lane < square_row, row_mass, 0.0), axis=1, keepdims=True)
    own = as_column(row_mass)
    drain(total.at[pl.ds(0, m - 1)], total_recv)
    rank = lax.broadcasted_iota(jnp.int32, (m, 1, LANES), 0)
    offset = jnp.sum(jnp.where(rank < ring, total[...], 0.0), axis=0)[:, :1]
    enclosed = star_mass + offset + before + 0.5 * own
    enclosed_out[...] = jnp.sum(jnp.where(square_row == square_lane, enclosed, 0.0), axis=0, keepdims=True)
    pull = as_column(gravity[...]) * enclosed

    tables[0] = jnp.broadcast_to(pull, (rows, LANES))
    tables[1] = jnp.broadcast_to(as_column(kappa_az[...]), (rows, LANES))
    tables[2] = jnp.broadcast_to(as_column(kappa_rad[...]), (rows, LANES))

    def wide(index, block):
        tile = tables[index, block * SUB:(block + 1) * SUB, :]
        return jnp.concatenate([tile] * (cols // LANES), axis=1)

    def pulled(block):
        at = slice(block * SUB, (block + 1) * SUB)
        rate = wide(0, block)
        for kind in (3, 1):
            lo, under = kind * layers, (kind // 2) * layers
            adv[lo:lo + layers, at, :] = adv[lo:lo + layers, at, :] - rate * adv[under:under + layers, at, :]

    def line_of(slab, block):
        index = ((per_slab - block) % per_slab) * slabs + slab
        chunk = index // n
        device = index % n if chunk < chunks - 1 else static_owner(index - n * chunk)
        return edge_in[chunk, device].reshape(1, 1, LANES)

    def static_owner(index):
        if n == 2 * last:
            return 2 * index + (index // 2 + index) % 2
        return (index * n + n - 1) // last

    block_row = lax.broadcasted_iota(jnp.int32, (slabs, SUB, cols), 1)
    block_lane = lax.broadcasted_iota(jnp.int32, (slabs, SUB, cols), 2)

    def diffused(block):
        low, high = block * SUB, (block + 1) * SUB
        here = adv[:, low:high, :]
        own_lines = jnp.concatenate([line_of(slab, block) for slab in range(slabs)], axis=0)
        none = jnp.zeros((1, 1, LANES), jnp.float32)
        under = []
        for slab in range(slabs):
            kind = slab // layers
            under.append(line_of(slab - (layers if kind == 1 else 2 * layers), block) if kind in (1, 3) else none)
        under = jnp.concatenate(under, axis=0)
        ends = own_lines - tables[0, low:high, :][None] * under
        left = jnp.sum(jnp.where((small == 0)[None], ends, 0.0), axis=2, keepdims=True)
        right = jnp.sum(jnp.where((small == SUB)[None], ends, 0.0), axis=2, keepdims=True)
        if block > 0:
            top = adv[:, low - 1:low, :]
        else:
            top = jnp.where(ring > 0, halo_in[3, :slabs, :], 0.0).reshape(slabs, 1, cols)
        if block < per_slab - 1:
            bottom = adv[:, high:high + 1, :]
        else:
            bottom = jnp.where(ring < m - 1, halo_in[2, :slabs, :], 0.0).reshape(slabs, 1, cols)
        lower = jnp.where(block_lane == 0, left, pltpu.roll(here, 1, axis=2))
        upper = jnp.where(block_lane == cols - 1, right, pltpu.roll(here, cols - 1, axis=2))
        above = jnp.where(block_row == 0, top, pltpu.roll(here, 1, axis=1))
        beneath = jnp.where(block_row == SUB - 1, bottom, pltpu.roll(here, SUB - 1, axis=1))
        twice = 2.0 * here
        out[:, low:high, :] = (
            here + wide(1, block)[None] * (lower + upper - twice)
            + wide(2, block)[None] * (beneath + above - twice)
        )

    def wait_halo():
        drain(halo_in.at[0], halo_recv.at[0])
        drain(halo_in.at[1], halo_recv.at[1])

    order = [(per_slab - turn) % per_slab for turn in range(per_slab)]
    ready, done = set(), set()
    state = 0
    for chunk in range(chunks):
        if chunk < chunks - 1:
            drain(pieces(n - 1), recv2.at[chunk])
            drain(lines(n - 1), edge_recv.at[chunk])
        else:
            wait_last(pieces, recv2.at[chunk])
            wait_last(lines, edge_recv.at[chunk])
        for block in order[len(ready):min(n * (chunk + 1), groups) // slabs]:
            pulled(block)
            ready.add(block)
        if state == 1:
            wait_halo()
            state = 2
        if state == 0 and len(ready) > 1:
            halo_in[0, :slabs, :] = adv[:, 0:1, :].reshape(slabs, cols)
            halo_in[1, :slabs, :] = adv[:, rows - 1:rows, :].reshape(slabs, cols)
            to_rad(halo_in.at[0], halo_in.at[2], halo_send.at[0], halo_recv.at[0], rad_peer(m - 1)).start()
            to_rad(halo_in.at[1], halo_in.at[3], halo_send.at[1], halo_recv.at[1], rad_peer(1)).start()
            state = 1
        if state == 1 and chunk == chunks - 1:
            wait_halo()
            state = 2
        for block in order:
            near = {block, max(block - 1, 0), min(block + 1, per_slab - 1)}
            rim = block in (0, per_slab - 1)
            if block not in done and near <= ready and (state == 2 or not rim):
                diffused(block)
                done.add(block)

    drain(mass.at[pl.ds(0, n - 1)], mass_send)
    drain(total.at[pl.ds(0, m - 1)], total_send)
    drain(halo_in.at[0], halo_send.at[0])
    drain(halo_in.at[1], halo_send.at[1])

    def wait_sent(chunk, _):
        drain(pieces(n - 1), send1.at[chunk])
        drain(pieces(n - 1), send2.at[chunk])
        drain(lines(n - 1), edge_send.at[chunk])
        return 0

    lax.fori_loop(0, chunks - 1, wait_sent, 0)
    wait_last(pieces, send1.at[chunks - 1])

    @pl.when(held)
    def _():
        drain(pieces(n - 1), send2.at[chunks - 1])
        drain(lines(n - 1), edge_send.at[chunks - 1])


def shards(n, m, fields, shifts, area, gravity, kappa_az, kappa_rad):
    kinds, layers, rows, cols = fields.shape
    slabs = kinds * layers
    chunks = -(-(slabs * (rows // SUB)) // n)
    line = (1, rows)
    f32 = jnp.float32
    dma = pltpu.SemaphoreType.DMA
    vmem = pl.BlockSpec(memory_space=pltpu.VMEM)
    hbm = pl.BlockSpec(memory_space=pltpu.HBM)
    slab_pad = -(-slabs // SUB) * SUB
    updated, enclosed = pl.pallas_call(
        functools.partial(kernel, n, m, layers),
        out_shape=(
            jax.ShapeDtypeStruct((slabs, rows, cols), f32),
            jax.ShapeDtypeStruct(line, f32),
        ),
        in_specs=[hbm] * 6,
        out_specs=(vmem, vmem),
        scratch_shapes=[
            pltpu.VMEM((slabs, rows, cols), f32),
            pltpu.VMEM(line, jnp.int32),
            pltpu.VMEM(line, f32), pltpu.VMEM(line, f32), pltpu.VMEM(line, f32), pltpu.VMEM(line, f32),
            dma((6,)),
            pltpu.VMEM((chunks, n, SUB, cols), f32),
            pltpu.VMEM((chunks, n, SUB, cols), f32),
            pltpu.VMEM((slabs, rows, cols), f32),
            pltpu.VMEM((chunks, n, 1, LANES), f32),
            pltpu.VMEM((chunks, n, 1, LANES), f32),
            pltpu.VMEM((n, 1, LANES), f32),
            pltpu.VMEM((m, 1, LANES), f32),
            pltpu.VMEM((rows, LANES), jnp.int32),
            pltpu.VMEM((3, rows, LANES), f32),
            pltpu.VMEM((4, slab_pad, cols), f32),
            dma((chunks,)), dma((chunks,)), dma((chunks,)), dma((chunks,)),
            dma, dma, dma, dma, dma((chunks,)), dma((chunks,)), dma((2,)), dma((2,)),
        ],
        compiler_params=pltpu.CompilerParams(
            collective_id=0, has_side_effects=True, vmem_limit_bytes=105 * 512 * 1024
        ),
    )(
        fields.reshape(slabs, rows, cols), shifts.reshape(line), area.reshape(line),
        gravity.reshape(line), kappa_az.reshape(line), kappa_rad.reshape(line),
    )
    return updated.reshape(fields.shape), enclosed.reshape(rows)


def solution(mesh):
    placed = (P(None, None, "rad", "az"), P("rad"), P("rad"), P("rad"), P("rad"), P("rad"))
    return jax.shard_map(
        functools.partial(shards, mesh.shape["az"], mesh.shape["rad"]),
        mesh=mesh,
        in_specs=placed,
        out_specs=(P(None, None, "rad", "az"), P("rad")),
        check_vma=False,
    )
```

```python
import functools

import jax
import jax.numpy as jnp
from jax import lax
from jax.experimental import pallas as pl
from jax.experimental.pallas import tpu as pltpu
from jax.sharding import PartitionSpec as P

MESH = pl.DeviceIdType.MESH
SUB = 8
LANES = 128
star_mass = 1.0


def kernel(
    n, m, layers,
    source, shifts_in, area_in, gravity_in, kappa_az_in, kappa_rad_in,
    out, enclosed_out,
    fields, shifts, area, gravity, kappa_az, kappa_rad, load_sem,
    win, wout, adv, edge_out, edge_in, mass, total, shift_table, tables, halo_in,
    send1, recv1, send2, recv2, mass_send, mass_recv, total_send, total_recv,
    edge_send, edge_recv, halo_send, halo_recv,
):
    slabs, rows, cols = fields.shape
    per_slab = rows // SUB
    groups = slabs * per_slab
    chunks = -(-groups // n)
    last = groups - n * (chunks - 1)
    me = lax.axis_index("az")
    ring = lax.axis_index("rad")

    def peer(step):
        return lax.rem(me + step, n)

    def rad_peer(step):
        return lax.rem(ring + step, m)

    def place(group):
        slab = lax.rem(group, slabs)
        block = lax.rem(per_slab - lax.div(group, slabs), per_slab)
        return slab, pl.ds(pl.multiple_of(block * SUB, SUB), SUB)

    def owner(index):
        if n == 2 * last:
            return 2 * index + lax.rem(lax.div(index, 2) + index, 2)
        return lax.div(index * n + n - 1, last)

    def last_of(device):
        index = lax.div(device * last, n)
        held = owner(index) == device
        return held, n * (chunks - 1) + index

    def to_peer(src, dst, send, recv, device):
        return pltpu.make_async_remote_copy(
            src_ref=src, dst_ref=dst, send_sem=send, recv_sem=recv,
            device_id={"az": device}, device_id_type=MESH,
        )

    def to_rad(src, dst, send, recv, device):
        return pltpu.make_async_remote_copy(
            src_ref=src, dst_ref=dst, send_sem=send, recv_sem=recv,
            device_id={"rad": device}, device_id_type=MESH,
        )

    def drain(ref, sem):
        pltpu.make_async_copy(ref, ref, sem).wait()

    def pieces(count):
        return win.at[0, pl.ds(0, count)]

    loads = [
        pltpu.make_async_copy(here, there, load_sem.at[i])
        for i, (here, there) in enumerate((
            (source, fields), (shifts_in, shifts), (area_in, area),
            (gravity_in, gravity), (kappa_az_in, kappa_az), (kappa_rad_in, kappa_rad),
        ))
    ]
    barrier = pltpu.get_barrier_semaphore()

    def greet(step, _):
        pl.semaphore_signal(barrier, inc=1, device_id={"az": peer(step)}, device_id_type=MESH)
        return 0

    def greet_rad(step, _):
        pl.semaphore_signal(barrier, inc=1, device_id={"rad": rad_peer(step)}, device_id_type=MESH)
        return 0

    lax.fori_loop(1, n, greet, 0)
    lax.fori_loop(1, m, greet_rad, 0)

    for load in loads:
        load.start()

    row_at = lax.broadcasted_iota(jnp.int32, (rows, LANES), 0)
    lane_at = lax.broadcasted_iota(jnp.int32, (rows, LANES), 1)
    square_row = lax.broadcasted_iota(jnp.int32, (rows, rows), 0)
    square_lane = lax.broadcasted_iota(jnp.int32, (rows, rows), 1)

    def as_column(line):
        return jnp.sum(jnp.where(square_row == square_lane, line, 0.0), axis=1, keepdims=True)

    pl.semaphore_wait(barrier, n - 1 + m - 1)

    def send_rows(chunk, _):
        def one(step, _):
            device = peer(step)
            slab, block = place(n * chunk + device)
            to_peer(
                source.at[slab, block], win.at[chunk, me], send1.at[chunk], recv1.at[chunk], device
            ).start()
            return 0

        return lax.fori_loop(1, n, one, 0)

    lax.fori_loop(0, chunks - 1, send_rows, 0)

    def send_last(step, _):
        device = peer(step)
        held, group = last_of(device)

        @pl.when(held)
        def _():
            slab, block = place(group)
            to_peer(
                source.at[slab, block], win.at[chunks - 1, me],
                send1.at[chunks - 1], recv1.at[chunks - 1], device,
            ).start()

        return 0

    lax.fori_loop(1, n, send_last, 0)

    for load in loads:
        load.wait()
    density = fields[0]
    for z in range(1, layers):
        density = density + fields[z]
    local = jnp.sum(density, axis=1, keepdims=True)
    mass[me] = jnp.sum(jnp.where(row_at == lane_at, local, 0.0), axis=0, keepdims=True)

    def send_mass(step, _):
        to_peer(mass.at[me], mass.at[me], mass_send, mass_recv, peer(step)).start()
        return 0

    lax.fori_loop(1, n, send_mass, 0)

    shift_column = as_column(shifts[...].astype(jnp.float32)).astype(jnp.int32)
    shift_rows = jnp.broadcast_to(shift_column, (rows, LANES))
    shift_table[...] = shift_rows

    cells = n * cols
    small = lax.broadcasted_iota(jnp.int32, (SUB, LANES), 1) - lax.broadcasted_iota(jnp.int32, (SUB, LANES), 0)

    def roll_chunk(chunk, group):
        slab, block = place(group)
        win[chunk, me] = fields[slab, block, :]
        amount = shift_table[block, :]
        amount = amount[:, :1]
        row = jnp.concatenate([win[chunk, i] for i in range(n)], axis=1)
        for bit in range((cells - 1).bit_length()):
            rolled = pltpu.roll(row, 1 << bit, axis=1)
            row = jnp.where((amount >> bit) & 1 == 1, rolled, row)
        for i in range(n):
            wout[chunk, i] = row[:, i * cols:(i + 1) * cols]
        adv[slab, block, :] = wout[chunk, me]

        def back(step, _):
            device = peer(step)
            to_peer(
                wout.at[chunk, device], adv.at[slab, block], send2.at[chunk], recv2.at[chunk], device
            ).start()
            return 0

        lax.fori_loop(1, n, back, 0)
        for i in range(n):
            low = (i * cols - 1) % cells
            high = (i * cols + cols) % cells
            ends = jnp.where(
                small == 0, row[:, low:low + 1],
                jnp.where(small == SUB, row[:, high:high + 1], 0.0),
            )
            edge_out[chunk, i] = jnp.sum(ends, axis=0, keepdims=True)
        edge_in[chunk, me] = edge_out[chunk, me]

        def back_edges(step, _):
            device = peer(step)
            to_peer(
                edge_out.at[chunk, device], edge_in.at[chunk, me],
                edge_send.at[chunk], edge_recv.at[chunk], device,
            ).start()
            return 0

        lax.fori_loop(1, n, back_edges, 0)

    def turn(chunk, _):
        drain(pieces(n - 1), recv1.at[chunk])
        roll_chunk(chunk, n * chunk + me)
        return 0

    lax.fori_loop(0, chunks - 1, turn, 0)
    held, group = last_of(me)

    @pl.when(held)
    def _():
        drain(pieces(n - 1), recv1.at[chunks - 1])
        roll_chunk(chunks - 1, group)

    def lines(count):
        return edge_in.at[0, pl.ds(0, count)]

    def wait_last(some, sem):
        @pl.when(held)
        def _():
            drain(some(last - 1), sem)

        @pl.when(jnp.logical_not(held))
        def _():
            drain(some(last), sem)

    drain(mass.at[pl.ds(0, n - 1)], mass_recv)
    cycle_mass = jnp.sum(mass[...], axis=0)[:, :rows]
    row_mass = area[...] * cycle_mass / (2.0 * (n * cols))
    block_mass = jnp.sum(row_mass, axis=1, keepdims=True)
    total[ring] = jnp.broadcast_to(block_mass, (1, LANES))

    def send_total(step, _):
        to_rad(total.at[ring], total.at[ring], total_send, total_recv, rad_peer(step)).start()
        return 0

    lax.fori_loop(1, m, send_total, 0)
    before = jnp.sum(jnp.where(square_lane < square_row, row_mass, 0.0), axis=1, keepdims=True)
    own = as_column(row_mass)
    drain(total.at[pl.ds(0, m - 1)], total_recv)
    rank = lax.broadcasted_iota(jnp.int32, (m, 1, LANES), 0)
    offset = jnp.sum(jnp.where(rank < ring, total[...], 0.0), axis=0)[:, :1]
    enclosed = star_mass + offset + before + 0.5 * own
    enclosed_out[...] = jnp.sum(jnp.where(square_row == square_lane, enclosed, 0.0), axis=0, keepdims=True)
    pull = as_column(gravity[...]) * enclosed

    tables[0] = jnp.broadcast_to(pull, (rows, LANES))
    tables[1] = jnp.broadcast_to(as_column(kappa_az[...]), (rows, LANES))
    tables[2] = jnp.broadcast_to(as_column(kappa_rad[...]), (rows, LANES))

    def wide(index, block):
        tile = tables[index, block * SUB:(block + 1) * SUB, :]
        return jnp.concatenate([tile] * (cols // LANES), axis=1)

    def pulled(block):
        at = slice(block * SUB, (block + 1) * SUB)
        rate = wide(0, block)
        for kind in (3, 1):
            lo, under = kind * layers, (kind // 2) * layers
            adv[lo:lo + layers, at, :] = adv[lo:lo + layers, at, :] - rate * adv[under:under + layers, at, :]

    def line_of(slab, block):
        index = ((per_slab - block) % per_slab) * slabs + slab
        chunk = index // n
        device = index % n if chunk < chunks - 1 else static_owner(index - n * chunk)
        return edge_in[chunk, device].reshape(1, 1, LANES)

    def static_owner(index):
        if n == 2 * last:
            return 2 * index + (index // 2 + index) % 2
        return (index * n + n - 1) // last

    block_row = lax.broadcasted_iota(jnp.int32, (slabs, SUB, cols), 1)
    block_lane = lax.broadcasted_iota(jnp.int32, (slabs, SUB, cols), 2)

    def diffused(block):
        low, high = block * SUB, (block + 1) * SUB
        here = adv[:, low:high, :]
        own_lines = jnp.concatenate([line_of(slab, block) for slab in range(slabs)], axis=0)
        none = jnp.zeros((1, 1, LANES), jnp.float32)
        under = []
        for slab in range(slabs):
            kind = slab // layers
            under.append(line_of(slab - (layers if kind == 1 else 2 * layers), block) if kind in (1, 3) else none)
        under = jnp.concatenate(under, axis=0)
        ends = own_lines - tables[0, low:high, :][None] * under
        left = jnp.sum(jnp.where((small == 0)[None], ends, 0.0), axis=2, keepdims=True)
        right = jnp.sum(jnp.where((small == SUB)[None], ends, 0.0), axis=2, keepdims=True)
        if block > 0:
            top = adv[:, low - 1:low, :]
        else:
            top = jnp.where(ring > 0, halo_in[3, :slabs, :], 0.0).reshape(slabs, 1, cols)
        if block < per_slab - 1:
            bottom = adv[:, high:high + 1, :]
        else:
            bottom = jnp.where(ring < m - 1, halo_in[2, :slabs, :], 0.0).reshape(slabs, 1, cols)
        lower = jnp.where(block_lane == 0, left, pltpu.roll(here, 1, axis=2))
        upper = jnp.where(block_lane == cols - 1, right, pltpu.roll(here, cols - 1, axis=2))
        above = jnp.where(block_row == 0, top, pltpu.roll(here, 1, axis=1))
        beneath = jnp.where(block_row == SUB - 1, bottom, pltpu.roll(here, SUB - 1, axis=1))
        twice = 2.0 * here
        out[:, low:high, :] = (
            here + wide(1, block)[None] * (lower + upper - twice)
            + wide(2, block)[None] * (beneath + above - twice)
        )

    def wait_halo():
        drain(halo_in.at[0], halo_recv.at[0])
        drain(halo_in.at[1], halo_recv.at[1])

    order = [(per_slab - turn) % per_slab for turn in range(per_slab)]
    ready, done = set(), set()
    state = 0
    for chunk in range(chunks):
        if chunk < chunks - 1:
            drain(pieces(n - 1), recv2.at[chunk])
            drain(lines(n - 1), edge_recv.at[chunk])
        else:
            wait_last(pieces, recv2.at[chunk])
            wait_last(lines, edge_recv.at[chunk])
        for block in order[len(ready):min(n * (chunk + 1), groups) // slabs]:
            pulled(block)
            ready.add(block)
        if state == 1:
            wait_halo()
            state = 2
        if state == 0 and len(ready) > 1:
            halo_in[0, :slabs, :] = adv[:, 0:1, :].reshape(slabs, cols)
            halo_in[1, :slabs, :] = adv[:, rows - 1:rows, :].reshape(slabs, cols)
            to_rad(halo_in.at[0], halo_in.at[2], halo_send.at[0], halo_recv.at[0], rad_peer(m - 1)).start()
            to_rad(halo_in.at[1], halo_in.at[3], halo_send.at[1], halo_recv.at[1], rad_peer(1)).start()
            state = 1
        if state == 1 and chunk == chunks - 1:
            wait_halo()
            state = 2
        for block in order:
            near = {block, max(block - 1, 0), min(block + 1, per_slab - 1)}
            rim = block in (0, per_slab - 1)
            if block not in done and near <= ready and (state == 2 or not rim):
                diffused(block)
                done.add(block)

    drain(mass.at[pl.ds(0, n - 1)], mass_send)
    drain(total.at[pl.ds(0, m - 1)], total_send)
    drain(halo_in.at[0], halo_send.at[0])
    drain(halo_in.at[1], halo_send.at[1])

    def wait_sent(chunk, _):
        drain(pieces(n - 1), send1.at[chunk])
        drain(pieces(n - 1), send2.at[chunk])
        drain(lines(n - 1), edge_send.at[chunk])
        return 0

    lax.fori_loop(0, chunks - 1, wait_sent, 0)
    wait_last(pieces, send1.at[chunks - 1])

    @pl.when(held)
    def _():
        drain(pieces(n - 1), send2.at[chunks - 1])
        drain(lines(n - 1), edge_send.at[chunks - 1])


def shards(n, m, fields, shifts, area, gravity, kappa_az, kappa_rad):
    kinds, layers, rows, cols = fields.shape
    slabs = kinds * layers
    chunks = -(-(slabs * (rows // SUB)) // n)
    line = (1, rows)
    f32 = jnp.float32
    dma = pltpu.SemaphoreType.DMA
    vmem = pl.BlockSpec(memory_space=pltpu.VMEM)
    hbm = pl.BlockSpec(memory_space=pltpu.HBM)
    slab_pad = -(-slabs // SUB) * SUB
    updated, enclosed = pl.pallas_call(
        functools.partial(kernel, n, m, layers),
        out_shape=(
            jax.ShapeDtypeStruct((slabs, rows, cols), f32),
            jax.ShapeDtypeStruct(line, f32),
        ),
        in_specs=[hbm] * 6,
        out_specs=(vmem, vmem),
        scratch_shapes=[
            pltpu.VMEM((slabs, rows, cols), f32),
            pltpu.VMEM(line, jnp.int32),
            pltpu.VMEM(line, f32), pltpu.VMEM(line, f32), pltpu.VMEM(line, f32), pltpu.VMEM(line, f32),
            dma((6,)),
            pltpu.VMEM((chunks, n, SUB, cols), f32),
            pltpu.VMEM((chunks, n, SUB, cols), f32),
            pltpu.VMEM((slabs, rows, cols), f32),
            pltpu.VMEM((chunks, n, 1, LANES), f32),
            pltpu.VMEM((chunks, n, 1, LANES), f32),
            pltpu.VMEM((n, 1, LANES), f32),
            pltpu.VMEM((m, 1, LANES), f32),
            pltpu.VMEM((rows, LANES), jnp.int32),
            pltpu.VMEM((3, rows, LANES), f32),
            pltpu.VMEM((4, slab_pad, cols), f32),
            dma((chunks,)), dma((chunks,)), dma((chunks,)), dma((chunks,)),
            dma, dma, dma, dma, dma((chunks,)), dma((chunks,)), dma((2,)), dma((2,)),
        ],
        compiler_params=pltpu.CompilerParams(
            collective_id=0, has_side_effects=True, vmem_limit_bytes=105 * 512 * 1024
        ),
    )(
        fields.reshape(slabs, rows, cols), shifts.reshape(line), area.reshape(line),
        gravity.reshape(line), kappa_az.reshape(line), kappa_rad.reshape(line),
    )
    return updated.reshape(fields.shape), enclosed.reshape(rows)


def solution(mesh):
    placed = (P(None, None, "rad", "az"), P("rad"), P("rad"), P("rad"), P("rad"), P("rad"))
    return jax.shard_map(
        functools.partial(shards, mesh.shape["az"], mesh.shape["rad"]),
        mesh=mesh,
        in_specs=placed,
        out_specs=(P(None, None, "rad", "az"), P("rad")),
        check_vma=False,
    )
```

```python
import functools

import jax
import jax.numpy as jnp
from jax import lax
from jax.experimental import pallas as pl
from jax.experimental.pallas import tpu as pltpu
from jax.sharding import PartitionSpec as P

MESH = pl.DeviceIdType.MESH
SUB = 8
LANES = 128
AHEAD = 4
star_mass = 1.0


def kernel(
    n, m, layers,
    source, shifts_in, area_in, gravity_in, kappa_az_in, kappa_rad_in,
    out, enclosed_out,
    fields, shifts, area, gravity, kappa_az, kappa_rad, load_sem,
    win, wout, adv, edge_out, edge_in, mass, total, shift_table, tables, halo_in,
    send1, recv1, send2, recv2, mass_send, mass_recv, total_send, total_recv,
    edge_send, edge_recv, halo_send, halo_recv,
):
    slabs, rows, cols = fields.shape
    per_slab = rows // SUB
    groups = slabs * per_slab
    chunks = -(-groups // n)
    last = groups - n * (chunks - 1)
    me = lax.axis_index("az")
    ring = lax.axis_index("rad")

    def peer(step):
        if n & (n - 1) == 0:
            return (me + step) & (n - 1)
        return lax.rem(me + step, n)

    def over(value, by):
        return (value * (2 ** 18 // by + 1)) >> 18 if groups < 2 ** 12 and by < 64 else lax.div(value, by)

    def rad_peer(step):
        return lax.rem(ring + step, m)

    def place(group):
        turn = over(group, slabs)
        slab = group - turn * slabs
        block = jnp.where(turn == 0, 0, per_slab - turn)
        return slab, pl.ds(pl.multiple_of(block * SUB, SUB), SUB)

    def owner(index):
        if n == 2 * last:
            return 2 * index + lax.rem(lax.div(index, 2) + index, 2)
        return lax.div(index * n + n - 1, last)

    def last_of(device):
        index = lax.div(device * last, n)
        held = owner(index) == device
        return held, n * (chunks - 1) + index

    def to_peer(src, dst, send, recv, device):
        return pltpu.make_async_remote_copy(
            src_ref=src, dst_ref=dst, send_sem=send, recv_sem=recv,
            device_id={"az": device}, device_id_type=MESH,
        )

    def to_rad(src, dst, send, recv, device):
        return pltpu.make_async_remote_copy(
            src_ref=src, dst_ref=dst, send_sem=send, recv_sem=recv,
            device_id={"rad": device}, device_id_type=MESH,
        )

    def drain(ref, sem):
        pltpu.make_async_copy(ref, ref, sem).wait()

    def pieces(count):
        return win.at[0, pl.ds(0, count)]

    loads = [
        pltpu.make_async_copy(here, there, load_sem.at[i])
        for i, (here, there) in enumerate((
            (source, fields), (shifts_in, shifts), (area_in, area),
            (gravity_in, gravity), (kappa_az_in, kappa_az), (kappa_rad_in, kappa_rad),
        ))
    ]
    barrier = pltpu.get_barrier_semaphore()

    def greet(step, _):
        pl.semaphore_signal(barrier, inc=1, device_id={"az": peer(step)}, device_id_type=MESH)
        return 0

    def greet_rad(step, _):
        pl.semaphore_signal(barrier, inc=1, device_id={"rad": rad_peer(step)}, device_id_type=MESH)
        return 0

    lax.fori_loop(1, n, greet, 0)
    lax.fori_loop(1, m, greet_rad, 0)

    for load in loads:
        load.start()

    row_at = lax.broadcasted_iota(jnp.int32, (rows, LANES), 0)
    lane_at = lax.broadcasted_iota(jnp.int32, (rows, LANES), 1)
    square_row = lax.broadcasted_iota(jnp.int32, (rows, rows), 0)
    square_lane = lax.broadcasted_iota(jnp.int32, (rows, rows), 1)

    def as_column(line):
        return jnp.sum(jnp.where(square_row == square_lane, line, 0.0), axis=1, keepdims=True)

    pl.semaphore_wait(barrier, n - 1 + m - 1)

    def send_rows(chunk, _):
        def one(step, _):
            device = peer(step)
            slab, block = place(n * chunk + device)
            to_peer(
                source.at[slab, block], win.at[chunk, me], send1.at[chunk], recv1.at[chunk], device
            ).start()
            return 0

        return lax.fori_loop(1, n, one, 0)

    ahead = min(AHEAD, chunks - 1)
    lax.fori_loop(0, ahead, send_rows, 0)

    def send_last(step, _):
        device = peer(step)
        held, group = last_of(device)

        @pl.when(held)
        def _():
            slab, block = place(group)
            to_peer(
                source.at[slab, block], win.at[chunks - 1, me],
                send1.at[chunks - 1], recv1.at[chunks - 1], device,
            ).start()

        return 0

    for load in loads:
        load.wait()
    density = fields[0]
    for z in range(1, layers):
        density = density + fields[z]
    local = jnp.sum(density, axis=1, keepdims=True)
    mass[me] = jnp.sum(jnp.where(row_at == lane_at, local, 0.0), axis=0, keepdims=True)

    def send_mass(step, _):
        to_peer(mass.at[me], mass.at[me], mass_send, mass_recv, peer(step)).start()
        return 0

    lax.fori_loop(1, n, send_mass, 0)

    shift_column = as_column(shifts[...].astype(jnp.float32)).astype(jnp.int32)
    shift_rows = jnp.broadcast_to(shift_column, (rows, LANES))
    shift_table[...] = shift_rows

    cells = n * cols
    small = lax.broadcasted_iota(jnp.int32, (SUB, LANES), 1) - lax.broadcasted_iota(jnp.int32, (SUB, LANES), 0)

    def roll_chunk(chunk, group):
        slab, block = place(group)
        win[chunk, me] = fields[slab, block, :]
        amount = shift_table[block, :]
        amount = amount[:, :1]
        row = jnp.concatenate([win[chunk, i] for i in range(n)], axis=1)
        for bit in range((cells - 1).bit_length()):
            rolled = pltpu.roll(row, 1 << bit, axis=1)
            row = jnp.where((amount >> bit) & 1 == 1, rolled, row)
        for i in range(n):
            wout[chunk, i] = row[:, i * cols:(i + 1) * cols]
        adv[slab, block, :] = wout[chunk, me]

        for i in range(n):
            low = (i * cols - 1) % cells
            high = (i * cols + cols) % cells
            ends = jnp.where(
                small == 0, row[:, low:low + 1],
                jnp.where(small == SUB, row[:, high:high + 1], 0.0),
            )
            edge_out[chunk, i] = jnp.sum(ends, axis=0, keepdims=True)
        edge_in[chunk, me] = edge_out[chunk, me]

        def back(step, _):
            device = peer(step)
            to_peer(
                wout.at[chunk, device], adv.at[slab, block], send2.at[chunk], recv2.at[chunk], device
            ).start()
            to_peer(
                edge_out.at[chunk, device], edge_in.at[chunk, me],
                edge_send.at[chunk], edge_recv.at[chunk], device,
            ).start()
            return 0

        lax.fori_loop(1, n, back, 0)

    def turn(chunk, _):
        drain(pieces(n - 1), recv1.at[chunk])
        roll_chunk(chunk, n * chunk + me)
        return 0

    def turn_and_send(chunk, _):
        turn(chunk, 0)
        return send_rows(chunk + ahead, 0)

    lax.fori_loop(0, chunks - 1 - ahead, turn_and_send, 0)
    lax.fori_loop(1, n, send_last, 0)
    lax.fori_loop(chunks - 1 - ahead, chunks - 1, turn, 0)
    held, group = last_of(me)

    @pl.when(held)
    def _():
        drain(pieces(n - 1), recv1.at[chunks - 1])
        roll_chunk(chunks - 1, group)

    def lines(count):
        return edge_in.at[0, pl.ds(0, count)]

    def wait_last(some, sem):
        @pl.when(held)
        def _():
            drain(some(last - 1), sem)

        @pl.when(jnp.logical_not(held))
        def _():
            drain(some(last), sem)

    drain(mass.at[pl.ds(0, n - 1)], mass_recv)
    cycle_mass = jnp.sum(mass[...], axis=0)[:, :rows]
    row_mass = area[...] * cycle_mass / (2.0 * (n * cols))
    block_mass = jnp.sum(row_mass, axis=1, keepdims=True)
    total[ring] = jnp.broadcast_to(block_mass, (1, LANES))

    def send_total(step, _):
        to_rad(total.at[ring], total.at[ring], total_send, total_recv, rad_peer(step)).start()
        return 0

    lax.fori_loop(1, m, send_total, 0)
    before = jnp.sum(jnp.where(square_lane < square_row, row_mass, 0.0), axis=1, keepdims=True)
    own = as_column(row_mass)
    drain(total.at[pl.ds(0, m - 1)], total_recv)
    rank = lax.broadcasted_iota(jnp.int32, (m, 1, LANES), 0)
    offset = jnp.sum(jnp.where(rank < ring, total[...], 0.0), axis=0)[:, :1]
    enclosed = star_mass + offset + before + 0.5 * own
    enclosed_out[...] = jnp.sum(jnp.where(square_row == square_lane, enclosed, 0.0), axis=0, keepdims=True)
    pull = as_column(gravity[...]) * enclosed

    tables[0] = jnp.broadcast_to(pull, (rows, LANES))
    tables[1] = jnp.broadcast_to(as_column(kappa_az[...]), (rows, LANES))
    tables[2] = jnp.broadcast_to(as_column(kappa_rad[...]), (rows, LANES))

    def wide(index, block):
        tile = tables[index, block * SUB:(block + 1) * SUB, :]
        return jnp.concatenate([tile] * (cols // LANES), axis=1)

    def pulled(block):
        at = slice(block * SUB, (block + 1) * SUB)
        rate = wide(0, block)
        for kind in (3, 1):
            lo, under = kind * layers, (kind // 2) * layers
            adv[lo:lo + layers, at, :] = adv[lo:lo + layers, at, :] - rate * adv[under:under + layers, at, :]

    def line_of(slab, block):
        index = ((per_slab - block) % per_slab) * slabs + slab
        chunk = index // n
        device = index % n if chunk < chunks - 1 else static_owner(index - n * chunk)
        return edge_in[chunk, device].reshape(1, 1, LANES)

    def static_owner(index):
        if n == 2 * last:
            return 2 * index + (index // 2 + index) % 2
        return (index * n + n - 1) // last

    block_row = lax.broadcasted_iota(jnp.int32, (slabs, SUB, cols), 1)
    block_lane = lax.broadcasted_iota(jnp.int32, (slabs, SUB, cols), 2)

    def diffused(block):
        low, high = block * SUB, (block + 1) * SUB
        here = adv[:, low:high, :]
        own_lines = jnp.concatenate([line_of(slab, block) for slab in range(slabs)], axis=0)
        none = jnp.zeros((1, 1, LANES), jnp.float32)
        under = []
        for slab in range(slabs):
            kind = slab // layers
            under.append(line_of(slab - (layers if kind == 1 else 2 * layers), block) if kind in (1, 3) else none)
        under = jnp.concatenate(under, axis=0)
        ends = own_lines - tables[0, low:high, :][None] * under
        left = jnp.sum(jnp.where((small == 0)[None], ends, 0.0), axis=2, keepdims=True)
        right = jnp.sum(jnp.where((small == SUB)[None], ends, 0.0), axis=2, keepdims=True)
        if block > 0:
            top = adv[:, low - 1:low, :]
        else:
            top = jnp.where(ring > 0, halo_in[3, :slabs, :], 0.0).reshape(slabs, 1, cols)
        if block < per_slab - 1:
            bottom = adv[:, high:high + 1, :]
        else:
            bottom = jnp.where(ring < m - 1, halo_in[2, :slabs, :], 0.0).reshape(slabs, 1, cols)
        lower = jnp.where(block_lane == 0, left, pltpu.roll(here, 1, axis=2))
        upper = jnp.where(block_lane == cols - 1, right, pltpu.roll(here, cols - 1, axis=2))
        above = jnp.where(block_row == 0, top, pltpu.roll(here, 1, axis=1))
        beneath = jnp.where(block_row == SUB - 1, bottom, pltpu.roll(here, SUB - 1, axis=1))
        twice = 2.0 * here
        out[:, low:high, :] = (
            here + wide(1, block)[None] * (lower + upper - twice)
            + wide(2, block)[None] * (beneath + above - twice)
        )

    def wait_halo():
        drain(halo_in.at[0], halo_recv.at[0])
        drain(halo_in.at[1], halo_recv.at[1])

    order = [(per_slab - turn) % per_slab for turn in range(per_slab)]
    ready, done = set(), set()
    state = 0
    for chunk in range(chunks):
        if chunk < chunks - 1:
            drain(pieces(n - 1), recv2.at[chunk])
            drain(lines(n - 1), edge_recv.at[chunk])
        else:
            wait_last(pieces, recv2.at[chunk])
            wait_last(lines, edge_recv.at[chunk])
        for block in order[len(ready):min(n * (chunk + 1), groups) // slabs]:
            pulled(block)
            ready.add(block)
        if state == 1:
            wait_halo()
            state = 2
        if state == 0 and len(ready) > 1:
            halo_in[0, :slabs, :] = adv[:, 0:1, :].reshape(slabs, cols)
            halo_in[1, :slabs, :] = adv[:, rows - 1:rows, :].reshape(slabs, cols)
            to_rad(halo_in.at[0], halo_in.at[2], halo_send.at[0], halo_recv.at[0], rad_peer(m - 1)).start()
            to_rad(halo_in.at[1], halo_in.at[3], halo_send.at[1], halo_recv.at[1], rad_peer(1)).start()
            state = 1
        if state == 1 and chunk == chunks - 1:
            wait_halo()
            state = 2
        for block in order:
            near = {block, max(block - 1, 0), min(block + 1, per_slab - 1)}
            rim = block in (0, per_slab - 1)
            if block not in done and near <= ready and (state == 2 or not rim):
                diffused(block)
                done.add(block)

    drain(mass.at[pl.ds(0, n - 1)], mass_send)
    drain(total.at[pl.ds(0, m - 1)], total_send)
    drain(halo_in.at[0], halo_send.at[0])
    drain(halo_in.at[1], halo_send.at[1])

    def wait_sent(chunk, _):
        drain(pieces(n - 1), send1.at[chunk])
        drain(pieces(n - 1), send2.at[chunk])
        drain(lines(n - 1), edge_send.at[chunk])
        return 0

    lax.fori_loop(0, chunks - 1, wait_sent, 0)
    wait_last(pieces, send1.at[chunks - 1])

    @pl.when(held)
    def _():
        drain(pieces(n - 1), send2.at[chunks - 1])
        drain(lines(n - 1), edge_send.at[chunks - 1])


def shards(n, m, fields, shifts, area, gravity, kappa_az, kappa_rad):
    kinds, layers, rows, cols = fields.shape
    slabs = kinds * layers
    chunks = -(-(slabs * (rows // SUB)) // n)
    line = (1, rows)
    f32 = jnp.float32
    dma = pltpu.SemaphoreType.DMA
    vmem = pl.BlockSpec(memory_space=pltpu.VMEM)
    hbm = pl.BlockSpec(memory_space=pltpu.HBM)
    slab_pad = -(-slabs // SUB) * SUB
    updated, enclosed = pl.pallas_call(
        functools.partial(kernel, n, m, layers),
        out_shape=(
            jax.ShapeDtypeStruct((slabs, rows, cols), f32),
            jax.ShapeDtypeStruct(line, f32),
        ),
        in_specs=[hbm] * 6,
        out_specs=(vmem, vmem),
        scratch_shapes=[
            pltpu.VMEM((slabs, rows, cols), f32),
            pltpu.VMEM(line, jnp.int32),
            pltpu.VMEM(line, f32), pltpu.VMEM(line, f32), pltpu.VMEM(line, f32), pltpu.VMEM(line, f32),
            dma((6,)),
            pltpu.VMEM((chunks, n, SUB, cols), f32),
            pltpu.VMEM((chunks, n, SUB, cols), f32),
            pltpu.VMEM((slabs, rows, cols), f32),
            pltpu.VMEM((chunks, n, 1, LANES), f32),
            pltpu.VMEM((chunks, n, 1, LANES), f32),
            pltpu.VMEM((n, 1, LANES), f32),
            pltpu.VMEM((m, 1, LANES), f32),
            pltpu.VMEM((rows, LANES), jnp.int32),
            pltpu.VMEM((3, rows, LANES), f32),
            pltpu.VMEM((4, slab_pad, cols), f32),
            dma((chunks,)), dma((chunks,)), dma((chunks,)), dma((chunks,)),
            dma, dma, dma, dma, dma((chunks,)), dma((chunks,)), dma((2,)), dma((2,)),
        ],
        compiler_params=pltpu.CompilerParams(
            collective_id=0, has_side_effects=True, vmem_limit_bytes=105 * 512 * 1024
        ),
    )(
        fields.reshape(slabs, rows, cols), shifts.reshape(line), area.reshape(line),
        gravity.reshape(line), kappa_az.reshape(line), kappa_rad.reshape(line),
    )
    return updated.reshape(fields.shape), enclosed.reshape(rows)


def solution(mesh):
    placed = (P(None, None, "rad", "az"), P("rad"), P("rad"), P("rad"), P("rad"), P("rad"))
    return jax.shard_map(
        functools.partial(shards, mesh.shape["az"], mesh.shape["rad"]),
        mesh=mesh,
        in_specs=placed,
        out_specs=(P(None, None, "rad", "az"), P("rad")),
        check_vma=False,
    )
```

```python
import functools

import jax
import jax.numpy as jnp
from jax import lax
from jax.experimental import pallas as pl
from jax.experimental.pallas import tpu as pltpu
from jax.sharding import PartitionSpec as P

MESH = pl.DeviceIdType.MESH
SUB = 8
LANES = 128
AHEAD = 4
star_mass = 1.0


def kernel(
    n, m, layers,
    source, shifts_in, area_in, gravity_in, kappa_az_in, kappa_rad_in,
    out, enclosed_out,
    fields, shifts, area, gravity, kappa_az, kappa_rad, load_sem,
    win, wout, adv, edge_out, edge_in, mass, total, shift_table, tables, halo_in,
    send1, recv1, send2, recv2, mass_send, mass_recv, total_send, total_recv,
    edge_send, edge_recv, halo_send, halo_recv,
):
    slabs, rows, cols = fields.shape
    per_slab = rows // SUB
    groups = slabs * per_slab
    chunks = -(-groups // n)
    last = groups - n * (chunks - 1)
    me = lax.axis_index("az")
    ring = lax.axis_index("rad")

    def peer(step):
        if n & (n - 1) == 0:
            return (me + step) & (n - 1)
        return lax.rem(me + step, n)

    def over(value, by):
        return (value * (2 ** 18 // by + 1)) >> 18 if groups < 2 ** 12 and by < 64 else lax.div(value, by)

    def rad_peer(step):
        return lax.rem(ring + step, m)

    def place(group):
        turn = over(group, slabs)
        slab = group - turn * slabs
        block = jnp.where(turn == 0, 0, per_slab - turn)
        return slab, pl.ds(pl.multiple_of(block * SUB, SUB), SUB)

    def owner(index):
        if n == 2 * last:
            return 2 * index + lax.rem(lax.div(index, 2) + index, 2)
        return lax.div(index * n + n - 1, last)

    def last_of(device):
        index = lax.div(device * last, n)
        held = owner(index) == device
        return held, n * (chunks - 1) + index

    def to_peer(src, dst, send, recv, device):
        return pltpu.make_async_remote_copy(
            src_ref=src, dst_ref=dst, send_sem=send, recv_sem=recv,
            device_id={"az": device}, device_id_type=MESH,
        )

    def to_rad(src, dst, send, recv, device):
        return pltpu.make_async_remote_copy(
            src_ref=src, dst_ref=dst, send_sem=send, recv_sem=recv,
            device_id={"rad": device}, device_id_type=MESH,
        )

    def drain(ref, sem):
        pltpu.make_async_copy(ref, ref, sem).wait()

    def pieces(count):
        return win.at[0, pl.ds(0, count)]

    loads = [
        pltpu.make_async_copy(here, there, load_sem.at[i])
        for i, (here, there) in enumerate((
            (source, fields), (shifts_in, shifts), (area_in, area),
            (gravity_in, gravity), (kappa_az_in, kappa_az), (kappa_rad_in, kappa_rad),
        ))
    ]
    barrier = pltpu.get_barrier_semaphore()

    def greet(step, _):
        pl.semaphore_signal(barrier, inc=1, device_id={"az": peer(step)}, device_id_type=MESH)
        return 0

    def greet_rad(step, _):
        pl.semaphore_signal(barrier, inc=1, device_id={"rad": rad_peer(step)}, device_id_type=MESH)
        return 0

    lax.fori_loop(1, n, greet, 0)
    lax.fori_loop(1, m, greet_rad, 0)

    for load in loads:
        load.start()

    row_at = lax.broadcasted_iota(jnp.int32, (rows, LANES), 0)
    lane_at = lax.broadcasted_iota(jnp.int32, (rows, LANES), 1)
    square_row = lax.broadcasted_iota(jnp.int32, (rows, rows), 0)
    square_lane = lax.broadcasted_iota(jnp.int32, (rows, rows), 1)

    def as_column(line):
        return jnp.sum(jnp.where(square_row == square_lane, line, 0.0), axis=1, keepdims=True)

    loads[0].wait()
    pl.semaphore_wait(barrier, n - 1 + m - 1)

    def send_rows(chunk, _):
        def one(step, _):
            device = peer(step)
            slab, block = place(n * chunk + device)
            to_peer(
                fields.at[slab, block], win.at[chunk, me], send1.at[chunk], recv1.at[chunk], device
            ).start()
            return 0

        return lax.fori_loop(1, n, one, 0)

    ahead = min(AHEAD, chunks - 1)
    lax.fori_loop(0, ahead, send_rows, 0)

    def send_last(step, _):
        device = peer(step)
        held, group = last_of(device)

        @pl.when(held)
        def _():
            slab, block = place(group)
            to_peer(
                fields.at[slab, block], win.at[chunks - 1, me],
                send1.at[chunks - 1], recv1.at[chunks - 1], device,
            ).start()

        return 0

    for load in loads[1:]:
        load.wait()
    density = fields[0]
    for z in range(1, layers):
        density = density + fields[z]
    local = jnp.sum(density, axis=1, keepdims=True)
    mass[me] = jnp.sum(jnp.where(row_at == lane_at, local, 0.0), axis=0, keepdims=True)

    def send_mass(step, _):
        to_peer(mass.at[me], mass.at[me], mass_send, mass_recv, peer(step)).start()
        return 0

    lax.fori_loop(1, n, send_mass, 0)

    shift_column = as_column(shifts[...].astype(jnp.float32)).astype(jnp.int32)
    shift_rows = jnp.broadcast_to(shift_column, (rows, LANES))
    shift_table[...] = shift_rows

    cells = n * cols
    small = lax.broadcasted_iota(jnp.int32, (SUB, LANES), 1) - lax.broadcasted_iota(jnp.int32, (SUB, LANES), 0)

    def roll_chunk(chunk, group):
        slab, block = place(group)
        win[chunk, me] = fields[slab, block, :]
        amount = shift_table[block, :]
        amount = amount[:, :1]
        row = jnp.concatenate([win[chunk, i] for i in range(n)], axis=1)
        for bit in range((cells - 1).bit_length()):
            rolled = pltpu.roll(row, 1 << bit, axis=1)
            row = jnp.where((amount >> bit) & 1 == 1, rolled, row)
        for i in range(n):
            wout[chunk, i] = row[:, i * cols:(i + 1) * cols]
        adv[slab, block, :] = wout[chunk, me]

        for i in range(n):
            low = (i * cols - 1) % cells
            high = (i * cols + cols) % cells
            ends = jnp.where(
                small == 0, row[:, low:low + 1],
                jnp.where(small == SUB, row[:, high:high + 1], 0.0),
            )
            edge_out[chunk, i] = jnp.sum(ends, axis=0, keepdims=True)
        edge_in[chunk, me] = edge_out[chunk, me]

        def back(step, _):
            device = peer(step)
            to_peer(
                wout.at[chunk, device], adv.at[slab, block], send2.at[chunk], recv2.at[chunk], device
            ).start()
            to_peer(
                edge_out.at[chunk, device], edge_in.at[chunk, me],
                edge_send.at[chunk], edge_recv.at[chunk], device,
            ).start()
            return 0

        lax.fori_loop(1, n, back, 0)

    def turn(chunk, _):
        drain(pieces(n - 1), recv1.at[chunk])
        roll_chunk(chunk, n * chunk + me)
        return 0

    def turn_and_send(chunk, _):
        turn(chunk, 0)
        return send_rows(chunk + ahead, 0)

    lax.fori_loop(0, chunks - 1 - ahead, turn_and_send, 0)
    lax.fori_loop(1, n, send_last, 0)
    lax.fori_loop(chunks - 1 - ahead, chunks - 1, turn, 0)
    held, group = last_of(me)

    @pl.when(held)
    def _():
        drain(pieces(n - 1), recv1.at[chunks - 1])
        roll_chunk(chunks - 1, group)

    def lines(count):
        return edge_in.at[0, pl.ds(0, count)]

    def wait_last(some, sem):
        @pl.when(held)
        def _():
            drain(some(last - 1), sem)

        @pl.when(jnp.logical_not(held))
        def _():
            drain(some(last), sem)

    drain(mass.at[pl.ds(0, n - 1)], mass_recv)
    cycle_mass = jnp.sum(mass[...], axis=0)[:, :rows]
    row_mass = area[...] * cycle_mass / (2.0 * (n * cols))
    block_mass = jnp.sum(row_mass, axis=1, keepdims=True)
    total[ring] = jnp.broadcast_to(block_mass, (1, LANES))

    def send_total(step, _):
        to_rad(total.at[ring], total.at[ring], total_send, total_recv, rad_peer(step)).start()
        return 0

    lax.fori_loop(1, m, send_total, 0)
    before = jnp.sum(jnp.where(square_lane < square_row, row_mass, 0.0), axis=1, keepdims=True)
    own = as_column(row_mass)
    drain(total.at[pl.ds(0, m - 1)], total_recv)
    rank = lax.broadcasted_iota(jnp.int32, (m, 1, LANES), 0)
    offset = jnp.sum(jnp.where(rank < ring, total[...], 0.0), axis=0)[:, :1]
    enclosed = star_mass + offset + before + 0.5 * own
    enclosed_out[...] = jnp.sum(jnp.where(square_row == square_lane, enclosed, 0.0), axis=0, keepdims=True)
    pull = as_column(gravity[...]) * enclosed

    tables[0] = jnp.broadcast_to(pull, (rows, LANES))
    tables[1] = jnp.broadcast_to(as_column(kappa_az[...]), (rows, LANES))
    tables[2] = jnp.broadcast_to(as_column(kappa_rad[...]), (rows, LANES))

    def wide(index, block):
        tile = tables[index, block * SUB:(block + 1) * SUB, :]
        return jnp.concatenate([tile] * (cols // LANES), axis=1)

    def pulled(block):
        at = slice(block * SUB, (block + 1) * SUB)
        rate = wide(0, block)
        for kind in (3, 1):
            lo, under = kind * layers, (kind // 2) * layers
            adv[lo:lo + layers, at, :] = adv[lo:lo + layers, at, :] - rate * adv[under:under + layers, at, :]

    def line_of(slab, block):
        index = ((per_slab - block) % per_slab) * slabs + slab
        chunk = index // n
        device = index % n if chunk < chunks - 1 else static_owner(index - n * chunk)
        return edge_in[chunk, device].reshape(1, 1, LANES)

    def static_owner(index):
        if n == 2 * last:
            return 2 * index + (index // 2 + index) % 2
        return (index * n + n - 1) // last

    block_row = lax.broadcasted_iota(jnp.int32, (slabs, SUB, cols), 1)
    block_lane = lax.broadcasted_iota(jnp.int32, (slabs, SUB, cols), 2)

    def diffused(block):
        low, high = block * SUB, (block + 1) * SUB
        here = adv[:, low:high, :]
        own_lines = jnp.concatenate([line_of(slab, block) for slab in range(slabs)], axis=0)
        none = jnp.zeros((1, 1, LANES), jnp.float32)
        under = []
        for slab in range(slabs):
            kind = slab // layers
            under.append(line_of(slab - (layers if kind == 1 else 2 * layers), block) if kind in (1, 3) else none)
        under = jnp.concatenate(under, axis=0)
        ends = own_lines - tables[0, low:high, :][None] * under
        left = jnp.sum(jnp.where((small == 0)[None], ends, 0.0), axis=2, keepdims=True)
        right = jnp.sum(jnp.where((small == SUB)[None], ends, 0.0), axis=2, keepdims=True)
        if block > 0:
            top = adv[:, low - 1:low, :]
        else:
            top = jnp.where(ring > 0, halo_in[3, :slabs, :], 0.0).reshape(slabs, 1, cols)
        if block < per_slab - 1:
            bottom = adv[:, high:high + 1, :]
        else:
            bottom = jnp.where(ring < m - 1, halo_in[2, :slabs, :], 0.0).reshape(slabs, 1, cols)
        lower = jnp.where(block_lane == 0, left, pltpu.roll(here, 1, axis=2))
        upper = jnp.where(block_lane == cols - 1, right, pltpu.roll(here, cols - 1, axis=2))
        above = jnp.where(block_row == 0, top, pltpu.roll(here, 1, axis=1))
        beneath = jnp.where(block_row == SUB - 1, bottom, pltpu.roll(here, SUB - 1, axis=1))
        twice = 2.0 * here
        out[:, low:high, :] = (
            here + wide(1, block)[None] * (lower + upper - twice)
            + wide(2, block)[None] * (beneath + above - twice)
        )

    def wait_halo():
        drain(halo_in.at[0], halo_recv.at[0])
        drain(halo_in.at[1], halo_recv.at[1])

    order = [(per_slab - turn) % per_slab for turn in range(per_slab)]
    ready, done = set(), set()
    state = 0
    for chunk in range(chunks):
        if chunk < chunks - 1:
            drain(pieces(n - 1), recv2.at[chunk])
            drain(lines(n - 1), edge_recv.at[chunk])
        else:
            wait_last(pieces, recv2.at[chunk])
            wait_last(lines, edge_recv.at[chunk])
        for block in order[len(ready):min(n * (chunk + 1), groups) // slabs]:
            pulled(block)
            ready.add(block)
        if state == 1:
            wait_halo()
            state = 2
        if state == 0 and len(ready) > 1:
            halo_in[0, :slabs, :] = adv[:, 0:1, :].reshape(slabs, cols)
            halo_in[1, :slabs, :] = adv[:, rows - 1:rows, :].reshape(slabs, cols)
            to_rad(halo_in.at[0], halo_in.at[2], halo_send.at[0], halo_recv.at[0], rad_peer(m - 1)).start()
            to_rad(halo_in.at[1], halo_in.at[3], halo_send.at[1], halo_recv.at[1], rad_peer(1)).start()
            state = 1
        if state == 1 and chunk == chunks - 1:
            wait_halo()
            state = 2
        for block in order:
            near = {block, max(block - 1, 0), min(block + 1, per_slab - 1)}
            rim = block in (0, per_slab - 1)
            if block not in done and near <= ready and (state == 2 or not rim):
                diffused(block)
                done.add(block)

    drain(mass.at[pl.ds(0, n - 1)], mass_send)
    drain(total.at[pl.ds(0, m - 1)], total_send)
    drain(halo_in.at[0], halo_send.at[0])
    drain(halo_in.at[1], halo_send.at[1])

    def wait_sent(chunk, _):
        drain(pieces(n - 1), send1.at[chunk])
        drain(pieces(n - 1), send2.at[chunk])
        drain(lines(n - 1), edge_send.at[chunk])
        return 0

    lax.fori_loop(0, chunks - 1, wait_sent, 0)
    wait_last(pieces, send1.at[chunks - 1])

    @pl.when(held)
    def _():
        drain(pieces(n - 1), send2.at[chunks - 1])
        drain(lines(n - 1), edge_send.at[chunks - 1])


def shards(n, m, fields, shifts, area, gravity, kappa_az, kappa_rad):
    kinds, layers, rows, cols = fields.shape
    slabs = kinds * layers
    chunks = -(-(slabs * (rows // SUB)) // n)
    line = (1, rows)
    f32 = jnp.float32
    dma = pltpu.SemaphoreType.DMA
    vmem = pl.BlockSpec(memory_space=pltpu.VMEM)
    hbm = pl.BlockSpec(memory_space=pltpu.HBM)
    slab_pad = -(-slabs // SUB) * SUB
    updated, enclosed = pl.pallas_call(
        functools.partial(kernel, n, m, layers),
        out_shape=(
            jax.ShapeDtypeStruct((slabs, rows, cols), f32),
            jax.ShapeDtypeStruct(line, f32),
        ),
        in_specs=[hbm] * 6,
        out_specs=(vmem, vmem),
        scratch_shapes=[
            pltpu.VMEM((slabs, rows, cols), f32),
            pltpu.VMEM(line, jnp.int32),
            pltpu.VMEM(line, f32), pltpu.VMEM(line, f32), pltpu.VMEM(line, f32), pltpu.VMEM(line, f32),
            dma((6,)),
            pltpu.VMEM((chunks, n, SUB, cols), f32),
            pltpu.VMEM((chunks, n, SUB, cols), f32),
            pltpu.VMEM((slabs, rows, cols), f32),
            pltpu.VMEM((chunks, n, 1, LANES), f32),
            pltpu.VMEM((chunks, n, 1, LANES), f32),
            pltpu.VMEM((n, 1, LANES), f32),
            pltpu.VMEM((m, 1, LANES), f32),
            pltpu.VMEM((rows, LANES), jnp.int32),
            pltpu.VMEM((3, rows, LANES), f32),
            pltpu.VMEM((4, slab_pad, cols), f32),
            dma((chunks,)), dma((chunks,)), dma((chunks,)), dma((chunks,)),
            dma, dma, dma, dma, dma((chunks,)), dma((chunks,)), dma((2,)), dma((2,)),
        ],
        compiler_params=pltpu.CompilerParams(
            collective_id=0, has_side_effects=True, vmem_limit_bytes=105 * 512 * 1024
        ),
    )(
        fields.reshape(slabs, rows, cols), shifts.reshape(line), area.reshape(line),
        gravity.reshape(line), kappa_az.reshape(line), kappa_rad.reshape(line),
    )
    return updated.reshape(fields.shape), enclosed.reshape(rows)


def solution(mesh):
    placed = (P(None, None, "rad", "az"), P("rad"), P("rad"), P("rad"), P("rad"), P("rad"))
    return jax.shard_map(
        functools.partial(shards, mesh.shape["az"], mesh.shape["rad"]),
        mesh=mesh,
        in_specs=placed,
        out_specs=(P(None, None, "rad", "az"), P("rad")),
        check_vma=False,
    )
```

```python
import functools

import jax
import jax.numpy as jnp
from jax import lax
from jax.experimental import pallas as pl
from jax.experimental.pallas import tpu as pltpu
from jax.sharding import PartitionSpec as P

MESH = pl.DeviceIdType.MESH
SUB = 8
LANES = 128
AHEAD = 4
star_mass = 1.0


def kernel(
    n, m, layers,
    source, shifts_in, area_in, gravity_in, kappa_az_in, kappa_rad_in,
    out, enclosed_out,
    fields, shifts, area, gravity, kappa_az, kappa_rad, load_sem,
    win, wout, adv, edge_out, edge_in, mass, total, shift_table, tables, halo_in,
    send1, recv1, send2, recv2, mass_send, mass_recv, total_send, total_recv,
    edge_send, edge_recv, halo_send, halo_recv,
):
    slabs, rows, cols = fields.shape
    per_slab = rows // SUB
    groups = slabs * per_slab
    chunks = -(-groups // n)
    last = groups - n * (chunks - 1)
    me = lax.axis_index("az")
    ring = lax.axis_index("rad")

    def peer(step):
        if n & (n - 1) == 0:
            return (me + 5 * step) & (n - 1)
        return lax.rem(me + step, n)

    def over(value, by):
        return (value * (2 ** 18 // by + 1)) >> 18 if groups < 2 ** 12 and by < 64 else lax.div(value, by)

    def rad_peer(step):
        return lax.rem(ring + step, m)

    def place(group):
        turn = over(group, slabs)
        slab = group - turn * slabs
        block = jnp.where(turn == 0, 0, per_slab - turn)
        return slab, pl.ds(pl.multiple_of(block * SUB, SUB), SUB)

    def owner(index):
        if n == 2 * last:
            return 2 * index + lax.rem(lax.div(index, 2) + index, 2)
        return lax.div(index * n + n - 1, last)

    def last_of(device):
        index = lax.div(device * last, n)
        held = owner(index) == device
        return held, n * (chunks - 1) + index

    def to_peer(src, dst, send, recv, device):
        return pltpu.make_async_remote_copy(
            src_ref=src, dst_ref=dst, send_sem=send, recv_sem=recv,
            device_id={"az": device}, device_id_type=MESH,
        )

    def to_rad(src, dst, send, recv, device):
        return pltpu.make_async_remote_copy(
            src_ref=src, dst_ref=dst, send_sem=send, recv_sem=recv,
            device_id={"rad": device}, device_id_type=MESH,
        )

    def drain(ref, sem):
        pltpu.make_async_copy(ref, ref, sem).wait()

    def pieces(count):
        return win.at[0, pl.ds(0, count)]

    loads = [
        pltpu.make_async_copy(here, there, load_sem.at[i])
        for i, (here, there) in enumerate((
            (source, fields), (shifts_in, shifts), (area_in, area),
            (gravity_in, gravity), (kappa_az_in, kappa_az), (kappa_rad_in, kappa_rad),
        ))
    ]
    barrier = pltpu.get_barrier_semaphore()

    def greet(step, _):
        pl.semaphore_signal(barrier, inc=1, device_id={"az": peer(step)}, device_id_type=MESH)
        return 0

    def greet_rad(step, _):
        pl.semaphore_signal(barrier, inc=1, device_id={"rad": rad_peer(step)}, device_id_type=MESH)
        return 0

    lax.fori_loop(1, n, greet, 0)
    lax.fori_loop(1, m, greet_rad, 0)

    for load in loads:
        load.start()

    row_at = lax.broadcasted_iota(jnp.int32, (rows, LANES), 0)
    lane_at = lax.broadcasted_iota(jnp.int32, (rows, LANES), 1)
    square_row = lax.broadcasted_iota(jnp.int32, (rows, rows), 0)
    square_lane = lax.broadcasted_iota(jnp.int32, (rows, rows), 1)

    def as_column(line):
        return jnp.sum(jnp.where(square_row == square_lane, line, 0.0), axis=1, keepdims=True)

    loads[0].wait()
    pl.semaphore_wait(barrier, n - 1 + m - 1)

    def send_rows(chunk, _):
        def one(step, _):
            device = peer(step)
            slab, block = place(n * chunk + device)
            to_peer(
                fields.at[slab, block], win.at[chunk, me], send1.at[chunk], recv1.at[chunk], device
            ).start()
            return 0

        return lax.fori_loop(1, n, one, 0)

    ahead = min(AHEAD, chunks - 1)
    lax.fori_loop(0, ahead, send_rows, 0)

    def send_last(step, _):
        device = peer(step)
        held, group = last_of(device)

        @pl.when(held)
        def _():
            slab, block = place(group)
            to_peer(
                fields.at[slab, block], win.at[chunks - 1, me],
                send1.at[chunks - 1], recv1.at[chunks - 1], device,
            ).start()

        return 0

    for load in loads[1:]:
        load.wait()
    density = fields[0]
    for z in range(1, layers):
        density = density + fields[z]
    local = jnp.sum(density, axis=1, keepdims=True)
    mass[me] = jnp.sum(jnp.where(row_at == lane_at, local, 0.0), axis=0, keepdims=True)

    def send_mass(step, _):
        to_peer(mass.at[me], mass.at[me], mass_send, mass_recv, peer(step)).start()
        return 0

    lax.fori_loop(1, n, send_mass, 0)

    shift_column = as_column(shifts[...].astype(jnp.float32)).astype(jnp.int32)
    shift_rows = jnp.broadcast_to(shift_column, (rows, LANES))
    shift_table[...] = shift_rows

    cells = n * cols
    small = lax.broadcasted_iota(jnp.int32, (SUB, LANES), 1) - lax.broadcasted_iota(jnp.int32, (SUB, LANES), 0)

    def roll_chunk(chunk, group):
        slab, block = place(group)
        win[chunk, me] = fields[slab, block, :]
        amount = shift_table[block, :]
        amount = amount[:, :1]
        row = jnp.concatenate([win[chunk, i] for i in range(n)], axis=1)
        for bit in range((cells - 1).bit_length()):
            rolled = pltpu.roll(row, 1 << bit, axis=1)
            row = jnp.where((amount >> bit) & 1 == 1, rolled, row)
        for i in range(n):
            wout[chunk, i] = row[:, i * cols:(i + 1) * cols]
        adv[slab, block, :] = wout[chunk, me]

        for i in range(n):
            low = (i * cols - 1) % cells
            high = (i * cols + cols) % cells
            ends = jnp.where(
                small == 0, row[:, low:low + 1],
                jnp.where(small == SUB, row[:, high:high + 1], 0.0),
            )
            edge_out[chunk, i] = jnp.sum(ends, axis=0, keepdims=True)
        edge_in[chunk, me] = edge_out[chunk, me]

        def back(step, _):
            device = peer(step)
            to_peer(
                wout.at[chunk, device], adv.at[slab, block], send2.at[chunk], recv2.at[chunk], device
            ).start()
            to_peer(
                edge_out.at[chunk, device], edge_in.at[chunk, me],
                edge_send.at[chunk], edge_recv.at[chunk], device,
            ).start()
            return 0

        lax.fori_loop(1, n, back, 0)

    def turn(chunk, _):
        drain(pieces(n - 1), recv1.at[chunk])
        roll_chunk(chunk, n * chunk + me)
        return 0

    def turn_and_send(chunk, _):
        turn(chunk, 0)
        return send_rows(chunk + ahead, 0)

    lax.fori_loop(0, chunks - 1 - ahead, turn_and_send, 0)
    lax.fori_loop(1, n, send_last, 0)
    lax.fori_loop(chunks - 1 - ahead, chunks - 1, turn, 0)
    held, group = last_of(me)

    @pl.when(held)
    def _():
        drain(pieces(n - 1), recv1.at[chunks - 1])
        roll_chunk(chunks - 1, group)

    def lines(count):
        return edge_in.at[0, pl.ds(0, count)]

    def wait_last(some, sem):
        @pl.when(held)
        def _():
            drain(some(last - 1), sem)

        @pl.when(jnp.logical_not(held))
        def _():
            drain(some(last), sem)

    drain(mass.at[pl.ds(0, n - 1)], mass_recv)
    cycle_mass = jnp.sum(mass[...], axis=0)[:, :rows]
    row_mass = area[...] * cycle_mass / (2.0 * (n * cols))
    block_mass = jnp.sum(row_mass, axis=1, keepdims=True)
    total[ring] = jnp.broadcast_to(block_mass, (1, LANES))

    def send_total(step, _):
        to_rad(total.at[ring], total.at[ring], total_send, total_recv, rad_peer(step)).start()
        return 0

    lax.fori_loop(1, m, send_total, 0)
    before = jnp.sum(jnp.where(square_lane < square_row, row_mass, 0.0), axis=1, keepdims=True)
    own = as_column(row_mass)
    drain(total.at[pl.ds(0, m - 1)], total_recv)
    rank = lax.broadcasted_iota(jnp.int32, (m, 1, LANES), 0)
    offset = jnp.sum(jnp.where(rank < ring, total[...], 0.0), axis=0)[:, :1]
    enclosed = star_mass + offset + before + 0.5 * own
    enclosed_out[...] = jnp.sum(jnp.where(square_row == square_lane, enclosed, 0.0), axis=0, keepdims=True)
    pull = as_column(gravity[...]) * enclosed

    tables[0] = jnp.broadcast_to(pull, (rows, LANES))
    tables[1] = jnp.broadcast_to(as_column(kappa_az[...]), (rows, LANES))
    tables[2] = jnp.broadcast_to(as_column(kappa_rad[...]), (rows, LANES))

    def wide(index, block):
        tile = tables[index, block * SUB:(block + 1) * SUB, :]
        return jnp.concatenate([tile] * (cols // LANES), axis=1)

    def pulled(block):
        at = slice(block * SUB, (block + 1) * SUB)
        rate = wide(0, block)
        for kind in (3, 1):
            lo, under = kind * layers, (kind // 2) * layers
            adv[lo:lo + layers, at, :] = adv[lo:lo + layers, at, :] - rate * adv[under:under + layers, at, :]

    def line_of(slab, block):
        index = ((per_slab - block) % per_slab) * slabs + slab
        chunk = index // n
        device = index % n if chunk < chunks - 1 else static_owner(index - n * chunk)
        return edge_in[chunk, device].reshape(1, 1, LANES)

    def static_owner(index):
        if n == 2 * last:
            return 2 * index + (index // 2 + index) % 2
        return (index * n + n - 1) // last

    block_row = lax.broadcasted_iota(jnp.int32, (slabs, SUB, cols), 1)
    block_lane = lax.broadcasted_iota(jnp.int32, (slabs, SUB, cols), 2)

    def diffused(block):
        low, high = block * SUB, (block + 1) * SUB
        here = adv[:, low:high, :]
        own_lines = jnp.concatenate([line_of(slab, block) for slab in range(slabs)], axis=0)
        none = jnp.zeros((1, 1, LANES), jnp.float32)
        under = []
        for slab in range(slabs):
            kind = slab // layers
            under.append(line_of(slab - (layers if kind == 1 else 2 * layers), block) if kind in (1, 3) else none)
        under = jnp.concatenate(under, axis=0)
        ends = own_lines - tables[0, low:high, :][None] * under
        left = jnp.sum(jnp.where((small == 0)[None], ends, 0.0), axis=2, keepdims=True)
        right = jnp.sum(jnp.where((small == SUB)[None], ends, 0.0), axis=2, keepdims=True)
        if block > 0:
            top = adv[:, low - 1:low, :]
        else:
            top = jnp.where(ring > 0, halo_in[3, :slabs, :], 0.0).reshape(slabs, 1, cols)
        if block < per_slab - 1:
            bottom = adv[:, high:high + 1, :]
        else:
            bottom = jnp.where(ring < m - 1, halo_in[2, :slabs, :], 0.0).reshape(slabs, 1, cols)
        lower = jnp.where(block_lane == 0, left, pltpu.roll(here, 1, axis=2))
        upper = jnp.where(block_lane == cols - 1, right, pltpu.roll(here, cols - 1, axis=2))
        above = jnp.where(block_row == 0, top, pltpu.roll(here, 1, axis=1))
        beneath = jnp.where(block_row == SUB - 1, bottom, pltpu.roll(here, SUB - 1, axis=1))
        twice = 2.0 * here
        out[:, low:high, :] = (
            here + wide(1, block)[None] * (lower + upper - twice)
            + wide(2, block)[None] * (beneath + above - twice)
        )

    def wait_halo():
        drain(halo_in.at[0], halo_recv.at[0])
        drain(halo_in.at[1], halo_recv.at[1])

    order = [(per_slab - turn) % per_slab for turn in range(per_slab)]
    ready, done = set(), set()
    state = 0
    for chunk in range(chunks):
        if chunk < chunks - 1:
            drain(pieces(n - 1), recv2.at[chunk])
            drain(lines(n - 1), edge_recv.at[chunk])
        else:
            wait_last(pieces, recv2.at[chunk])
            wait_last(lines, edge_recv.at[chunk])
        for block in order[len(ready):min(n * (chunk + 1), groups) // slabs]:
            pulled(block)
            ready.add(block)
        if state == 1:
            wait_halo()
            state = 2
        if state == 0 and len(ready) > 1:
            halo_in[0, :slabs, :] = adv[:, 0:1, :].reshape(slabs, cols)
            halo_in[1, :slabs, :] = adv[:, rows - 1:rows, :].reshape(slabs, cols)
            to_rad(halo_in.at[0], halo_in.at[2], halo_send.at[0], halo_recv.at[0], rad_peer(m - 1)).start()
            to_rad(halo_in.at[1], halo_in.at[3], halo_send.at[1], halo_recv.at[1], rad_peer(1)).start()
            state = 1
        if state == 1 and chunk == chunks - 1:
            wait_halo()
            state = 2
        for block in order:
            near = {block, max(block - 1, 0), min(block + 1, per_slab - 1)}
            rim = block in (0, per_slab - 1)
            if block not in done and near <= ready and (state == 2 or not rim):
                diffused(block)
                done.add(block)

    drain(mass.at[pl.ds(0, n - 1)], mass_send)
    drain(total.at[pl.ds(0, m - 1)], total_send)
    drain(halo_in.at[0], halo_send.at[0])
    drain(halo_in.at[1], halo_send.at[1])

    def wait_sent(chunk, _):
        drain(pieces(n - 1), send1.at[chunk])
        drain(pieces(n - 1), send2.at[chunk])
        drain(lines(n - 1), edge_send.at[chunk])
        return 0

    lax.fori_loop(0, chunks - 1, wait_sent, 0)
    wait_last(pieces, send1.at[chunks - 1])

    @pl.when(held)
    def _():
        drain(pieces(n - 1), send2.at[chunks - 1])
        drain(lines(n - 1), edge_send.at[chunks - 1])


def shards(n, m, fields, shifts, area, gravity, kappa_az, kappa_rad):
    kinds, layers, rows, cols = fields.shape
    slabs = kinds * layers
    chunks = -(-(slabs * (rows // SUB)) // n)
    line = (1, rows)
    f32 = jnp.float32
    dma = pltpu.SemaphoreType.DMA
    vmem = pl.BlockSpec(memory_space=pltpu.VMEM)
    hbm = pl.BlockSpec(memory_space=pltpu.HBM)
    slab_pad = -(-slabs // SUB) * SUB
    updated, enclosed = pl.pallas_call(
        functools.partial(kernel, n, m, layers),
        out_shape=(
            jax.ShapeDtypeStruct((slabs, rows, cols), f32),
            jax.ShapeDtypeStruct(line, f32),
        ),
        in_specs=[hbm] * 6,
        out_specs=(vmem, vmem),
        scratch_shapes=[
            pltpu.VMEM((slabs, rows, cols), f32),
            pltpu.VMEM(line, jnp.int32),
            pltpu.VMEM(line, f32), pltpu.VMEM(line, f32), pltpu.VMEM(line, f32), pltpu.VMEM(line, f32),
            dma((6,)),
            pltpu.VMEM((chunks, n, SUB, cols), f32),
            pltpu.VMEM((chunks, n, SUB, cols), f32),
            pltpu.VMEM((slabs, rows, cols), f32),
            pltpu.VMEM((chunks, n, 1, LANES), f32),
            pltpu.VMEM((chunks, n, 1, LANES), f32),
            pltpu.VMEM((n, 1, LANES), f32),
            pltpu.VMEM((m, 1, LANES), f32),
            pltpu.VMEM((rows, LANES), jnp.int32),
            pltpu.VMEM((3, rows, LANES), f32),
            pltpu.VMEM((4, slab_pad, cols), f32),
            dma((chunks,)), dma((chunks,)), dma((chunks,)), dma((chunks,)),
            dma, dma, dma, dma, dma((chunks,)), dma((chunks,)), dma((2,)), dma((2,)),
        ],
        compiler_params=pltpu.CompilerParams(
            collective_id=0, has_side_effects=True, vmem_limit_bytes=105 * 512 * 1024
        ),
    )(
        fields.reshape(slabs, rows, cols), shifts.reshape(line), area.reshape(line),
        gravity.reshape(line), kappa_az.reshape(line), kappa_rad.reshape(line),
    )
    return updated.reshape(fields.shape), enclosed.reshape(rows)


def solution(mesh):
    placed = (P(None, None, "rad", "az"), P("rad"), P("rad"), P("rad"), P("rad"), P("rad"))
    return jax.shard_map(
        functools.partial(shards, mesh.shape["az"], mesh.shape["rad"]),
        mesh=mesh,
        in_specs=placed,
        out_specs=(P(None, None, "rad", "az"), P("rad")),
        check_vma=False,
    )
```
